512 devices in a mesh: replica: 32 (over x, z_hi, core), fsdp: 16 (over z_lo, y).
Axes of the slice: x: 4, y: 4, z: 16 (z_hi: 4, z_lo: 4; z = z_hi * 4 + z_lo), core: 2. Of those that a mesh axis runs over, the one named last changes fastest.
Arguments:
- hidden: bfloat16 [32, 2048, 4608], P('replica', 'fsdp'), may hold values from -6 to 6
- queries: bfloat16 [32, 2048, 2048], P('replica', 'fsdp'), may hold values from -48 to 48
- values: bfloat16 [32, 2048, 1024], P('replica', 'fsdp'), may hold values from -6 to 6
- codes: bfloat16 [32, 4608, 1024], P('replica', 'fsdp'), may hold values from -6 to 6
- exponents: int32 [32, 4608, 8], P('replica', 'fsdp'), may hold values from -2 to 1
- base: bfloat16 [4608, 1024], P('fsdp'), may hold values from -1.5 to 1.5
- momentum: bfloat16 [4608, 1024], P('fsdp'), may hold values from -1.5 to 1.5
Outputs:
- blended: bfloat16 [32, 4608, 1024], P('replica', 'fsdp')
- attended: bfloat16 [32, 2048, 2048], P('replica', 'fsdp')
The draws below stay inside these ranges and needn't reach their ends.
All inputs are finite; a program needn't handle non-finite values.
Results may differ from the reference program's by a relative error of at most 0.035.
Values may be sent and summed in bfloat16 or wider, within the bound.
No kernel may reach another device: no remote copies, remote signals or barrier semaphores. Data moves between devices by JAX's collectives and lax.ppermute only.
A program may use at most 64 MiB of HBM per device.

```python
import math
import jax
import jax.numpy as jnp
from jax import lax

D = 4608
HD = 128
QH = 16
KVH = 8
BLOCK = 128
KC = 1024
TOKENS = 2048
REPLICAS = 32


def draw_queries(key, part):
    key = jax.random.fold_in(key, 11)
    key_core, key_level = jax.random.split(key)
    core = jnp.clip(jax.random.normal(key_core, (REPLICAS, TOKENS, QH, HD), jnp.float32), -4.0, 4.0)
    level = jax.random.uniform(key_level, (REPLICAS, TOKENS, QH, 1), jnp.float32, 0.0, math.log(12.0))
    return (core * jnp.exp(level)).reshape(REPLICAS, TOKENS, QH * HD).astype(jnp.bfloat16)


def with_ends(drawn, key, smallest, largest):
    extent = drawn.shape
    index_at = [jax.random.randint(jax.random.fold_in(key, axis), (), 0, extent[axis]) for axis in range(len(extent))]
    drawn = drawn.at[tuple(index_at)].set(smallest)
    longest = extent.index(max(extent))
    index_at[longest] = (index_at[longest] + 1) % extent[longest]
    return drawn.at[tuple(index_at)].set(largest)


def with_spikes(array, own_key, source, target, blocks, factor):
    def block_of(dim):
        return (jnp.arange(array.shape[dim]) // (array.shape[dim] // blocks)).reshape((-1,) + (1,) * (array.ndim - 1 - dim))

    near = jax.random.permutation(own_key, blocks)[block_of(target)]
    far = (block_of(target) + blocks // 2) % blocks
    return jnp.where((block_of(source) == near) | (block_of(source) == far), factor * array, array)


def level_of(own_key, shape, cuts, smallest, largest):
    level = 1.0
    for dim, shards_of in cuts:
        heights = jax.random.uniform(jax.random.fold_in(jax.random.fold_in(own_key, 6), dim), (shards_of,), jnp.float32, smallest / len(cuts), largest / len(cuts))
        level = level * jnp.repeat(jnp.exp(heights), shape[dim] // shards_of).reshape((-1,) + (1,) * (len(shape) - 1 - dim))
    return level


def gaussian(stream_key, extent, scale, bound, shards=(), dtype=jnp.bfloat16):
    gain = level_of(stream_key, extent, shards, -0.22, 0.18) if shards else 1.0
    drawn = jax.random.normal(stream_key, extent, jnp.float32) * scale * gain
    return jnp.minimum(jnp.maximum(drawn, -bound), bound).astype(dtype)


def bell_draw_with(own_key, dims, scale, reach, cuts, heavy, held_as=jnp.bfloat16):
    array = scale * jax.random.normal(own_key, dims, jnp.float32)
    if cuts:
        array = array * level_of(own_key, dims, cuts, -0.22, 0.18)
    return jnp.clip(with_spikes(array, jax.random.fold_in(own_key, 3), *heavy), -reach, reach).astype(held_as)


def setup_inputs(seed: int = 0) -> dict:
    splits = jax.random.split(jax.random.key(seed), 8)
    hidden = gaussian(splits[0], (REPLICAS, TOKENS, D), 1.0, 6.0, ((0, 32), (1, 16)))
    queries = draw_queries(jax.random.fold_in(splits[7], 71), 0)
    values = gaussian(splits[2], (REPLICAS, TOKENS, KC), 1.0, 6.0, ((0, 32), (1, 16)))
    codes = bell_draw_with(splits[3], (REPLICAS, D, KC), 1.0, 6.0, ((0, 32), (1, 16)), (0, 1, 32, 2.75))
    exponents = with_ends(jax.random.randint(splits[4], (REPLICAS, D, KC // BLOCK), -2, 2), jax.random.fold_in(splits[4], 1), -2, 1).astype(jnp.int32)
    base = gaussian(splits[5], (D, KC), 0.25, 1.5, ((0, 16),))
    momentum = gaussian(splits[6], (D, KC), 0.25, 1.5, ((0, 16),))
    return dict(hidden=hidden, queries=queries, values=values, codes=codes, exponents=exponents, base=base, momentum=momentum)


momentum_rate = 0.9
outer_rate = 0.7
blend_share = 0.25
logit_cap = 50.0
query_scalar = 12.0

def dequantize(code_block, exponent_block):
    row_count = code_block.shape[0]
    col_count = code_block.shape[1]
    factor = jnp.exp2(exponent_block.astype(jnp.float32))
    grouped = code_block.astype(jnp.float32).reshape(row_count, col_count // BLOCK, BLOCK)
    return (grouped * factor[:, :, None]).reshape(row_count, col_count)

def widen_heads(block):
    row_count = block.shape[0]
    group_size = QH // KVH
    spread = jnp.broadcast_to(block.reshape(row_count, KVH, 1, HD), (row_count, KVH, group_size, HD))
    return spread.reshape(row_count, QH * HD)

def attend(queries, key_rows, values):
    row_count = queries.shape[0]
    query_heads = jnp.transpose(queries.reshape(row_count, QH, HD), (1, 0, 2))
    key_heads = jnp.transpose(widen_heads(key_rows).reshape(row_count, QH, HD), (1, 0, 2))
    value_heads = jnp.transpose(widen_heads(values).reshape(row_count, QH, HD), (1, 0, 2))
    position = jnp.arange(row_count)
    allowed = position[None, :] <= position[:, None]

    def one_head(operands):
        query_one, key_one, value_one = operands
        scores = jnp.dot(query_one, key_one.T, preferred_element_type=jnp.float32) / query_scalar
        capped = logit_cap * jnp.tanh(scores / logit_cap)
        weights = jnp.where(allowed, jnp.exp(capped), jnp.zeros_like(capped))
        totals = lax.optimization_barrier(jnp.sum(weights, axis=1))
        mixed = jnp.dot(weights.astype(jnp.bfloat16), value_one, preferred_element_type=jnp.float32)
        return (mixed / totals[:, None]).astype(jnp.bfloat16)
    mixed_all = lax.map(one_head, (query_heads, key_heads, value_heads))
    return jnp.transpose(mixed_all, (1, 0, 2)).reshape(row_count, QH * HD)

def reference(hidden, queries, values, codes, exponents, base, momentum):

    def accumulate(summed, operands):
        return (summed + dequantize(operands[0], operands[1]), jnp.zeros((), jnp.float32))
    delta_total = lax.scan(accumulate, jnp.zeros((D, KC), jnp.float32), (codes, exponents))[0]
    mean_delta = delta_total / REPLICAS
    moment_new = momentum_rate * momentum.astype(jnp.float32) + mean_delta
    outer_params = (base.astype(jnp.float32) - outer_rate * (mean_delta + momentum_rate * moment_new)).astype(jnp.bfloat16)

    def one_replica(operands):
        rows_in, query_rows, value_rows, code_block, exponent_block = operands
        local_params = base.astype(jnp.float32) - dequantize(code_block, exponent_block)
        mixed_params = (blend_share * local_params + (1.0 - blend_share) * outer_params.astype(jnp.float32)).astype(jnp.bfloat16)
        key_rows = (jnp.dot(rows_in, mixed_params, preferred_element_type=jnp.float32) / math.sqrt(D)).astype(jnp.bfloat16)
        return (mixed_params, attend(query_rows, key_rows, value_rows))
    blended, attended = lax.map(one_replica, (hidden, queries, values, codes, exponents))
    return (blended, attended)
```

```python
import math

import jax
import jax.numpy as jnp
from jax import lax
from jax.experimental import pallas as pl
from jax.experimental.pallas import tpu as pltpu
from jax.sharding import Mesh
from jax.sharding import PartitionSpec as P

D = 4608
HD = 128
QH = 16
KVH = 8
BLOCK = 128
KC = 1024
VMEM = pl.BlockSpec(memory_space=pltpu.VMEM)
SMEM = pl.BlockSpec(memory_space=pltpu.SMEM)

momentum_rate = 0.9
outer_rate = 0.7
blend_share = 0.25
logit_cap = 50.0
query_scalar = 12.0

NX, NZH, NC, NZL, NY = 4, 4, 2, 4, 4


def params(mib=40):
    return pltpu.CompilerParams(vmem_limit_bytes=mib << 20)


def prep_kernel(codes_ref, exps_ref, base_ref, delta_ref, part_ref):
    factor = jnp.exp2(exps_ref[...].astype(jnp.float32))
    for j in range(KC // BLOCK):
        cols = slice(j * BLOCK, (j + 1) * BLOCK)
        delta = codes_ref[:, cols].astype(jnp.float32) * factor[:, j : j + 1]
        delta_ref[j] = delta.astype(jnp.bfloat16)
        part_ref[:, cols] = (base_ref[:, cols].astype(jnp.float32) - delta).astype(jnp.bfloat16)


def prep(codes, exps, base):
    rows = codes.shape[0]
    return pl.pallas_call(
        prep_kernel,
        out_shape=(
            jax.ShapeDtypeStruct((KC // BLOCK, rows, BLOCK), jnp.bfloat16),
            jax.ShapeDtypeStruct((rows, KC), jnp.bfloat16),
        ),
        in_specs=[VMEM] * 3,
        out_specs=(VMEM, VMEM),
        compiler_params=params(),
        name="prep",
    )(codes, exps, base)


def local_kernel(h0_ref, h1_ref, h2_ref, h3_ref, part_ref, hidden_ref, out_ref):
    for s, ref in enumerate((h0_ref, h1_ref, h2_ref, h3_ref)):
        hidden_ref[s * 128 : (s + 1) * 128, :] = ref[...]
    for n in range(KC // 256):
        cols = slice(n * 256, (n + 1) * 256)
        out_ref[:, cols] = blend_share * jnp.dot(
            hidden_ref[...], part_ref[:, cols], preferred_element_type=jnp.float32
        )


def local_product(hidden, part):
    return pl.pallas_call(
        local_kernel,
        out_shape=(
            jax.ShapeDtypeStruct((512, part.shape[0]), jnp.bfloat16),
            jax.ShapeDtypeStruct((512, KC), jnp.float32),
        ),
        in_specs=[VMEM] * 5,
        out_specs=(VMEM, VMEM),
        compiler_params=params(),
        name="local_product",
    )(*hidden, part)


def project_kernel(place_ref, hidden_ref, local_ref, same_ref, other_ref, out_ref, own_ref, weight):
    rows = own_ref.shape[0]
    c, z, y = place_ref[0], place_ref[1], place_ref[2]
    for x in range(NX):
        for near, ref in enumerate((same_ref, other_ref)):
            at = (x * NC + lax.rem(c + near, NC)) * BLOCK
            cols = pl.ds(pl.multiple_of(at, BLOCK), BLOCK)
            own_ref[:, cols] = ref[x * NY + y]
            for ys in range(NY):
                weight[ys * rows : (ys + 1) * rows, cols] = ref[x * NY + ys]
    for n in range(NZL):
        cols = slice(n * 256, (n + 1) * 256)
        outer = jnp.dot(hidden_ref[...], weight[:, cols], preferred_element_type=jnp.float32)
        total = (local_ref[:, cols] + (1.0 - blend_share) * outer).astype(jnp.bfloat16)
        for s in range(NZL):
            at = pl.multiple_of(lax.rem(z - s + NZL, NZL) * 128, 128)
            out_ref[n, pl.ds(at, 128), :] = total[s * 128 : (s + 1) * 128]


def project(place, hidden, local, same, other):
    rows = same.shape[1]
    return pl.pallas_call(
        project_kernel,
        out_shape=(
            jax.ShapeDtypeStruct((NZL, 512, KC // NZL), jnp.bfloat16),
            jax.ShapeDtypeStruct((rows, KC), jnp.bfloat16),
        ),
        in_specs=[SMEM] + [VMEM] * 4,
        out_specs=(VMEM, VMEM),
        scratch_shapes=[pltpu.VMEM((NY * rows, KC), jnp.bfloat16)],
        compiler_params=params(),
        name="project",
    )(place, hidden, local, same, other)


def attend_kernel(place_ref, q_ref, keys, values, out_ref):
    z, y = place_ref[1], place_ref[2]
    row = lax.broadcasted_iota(jnp.int32, (256, 128), 0) % 128
    col = lax.broadcasted_iota(jnp.int32, (256, 128), 1)
    seen = col - row
    for zq in range(NZL):
        at = lax.rem(z - zq + NZL, NZL)
        q = jnp.concatenate([q_ref[at, :, :HD], q_ref[at, :, HD:]], axis=0)
        acc = jnp.zeros((256, HD), jnp.float32)
        total = jnp.zeros((256, 128), jnp.float32)
        for zk in range(zq + 1):
            rows = slice(zk * 128, (zk + 1) * 128)
            value_rows = pl.ds(pl.multiple_of(lax.rem(z - zk + NZL, NZL) * 128, 128), 128)
            for s in range(NY):
                scores = lax.dot_general(
                    q,
                    keys[s, rows, :],
                    (((1,), (1,)), ((), ())),
                    preferred_element_type=jnp.float32,
                )
                p = jnp.exp(logit_cap * jnp.tanh(scores * (1.0 / (query_scalar * logit_cap))))
                if zk == zq:
                    p = jnp.where(seen <= (y - s) * 128, p, 0.0)
                total += p
                acc += jnp.dot(
                    p.astype(jnp.bfloat16),
                    values[s, value_rows, :],
                    preferred_element_type=jnp.float32,
                )
        out = (acc / jnp.sum(total, axis=1, keepdims=True)).astype(jnp.bfloat16)
        out_ref[zq, :, :HD] = out[:128]
        out_ref[zq, :, HD:] = out[128:]


def attend(place, q, keys, values):
    kv_spec = pl.BlockSpec((NY, 512, HD), lambda h: (0, 0, h))
    q_spec = pl.BlockSpec((NZL, 128, 2 * HD), lambda h: (0, 0, h))
    return pl.pallas_call(
        attend_kernel,
        grid=(2,),
        out_shape=jax.ShapeDtypeStruct((NZL, 128, 4 * HD), jnp.bfloat16),
        in_specs=[SMEM, q_spec] + [kv_spec] * 2,
        out_specs=q_spec,
        compiler_params=params(),
        name="attend",
    )(place, q, keys, values)


def swap(array, axis, pairs):
    return lax.ppermute(array, axis, pairs + [(b, a) for a, b in pairs])


def add(a, b):
    return a.astype(jnp.float32) + b.astype(jnp.float32)


def deal(arrays, axis):
    at = lax.axis_index(axis)
    pieces = []
    for step in range(4):
        to = lax.rem(at + step, 4)
        cut = []
        for array in arrays:
            width = array.shape[1] // 4
            cut.append(lax.dynamic_slice_in_dim(array, to * width, width, 1))
        piece = jnp.concatenate(cut, axis=1)
        if step:
            piece = lax.ppermute(piece, axis, [(i, (i + step) % 4) for i in range(4)])
        pieces.append(piece)
    return pieces


def gather(array, axis, size):
    return lax.all_to_all(jnp.broadcast_to(array, (size,) + array.shape), axis, 0, 0, tiled=True)


def exchange(array, axis):
    return lax.all_to_all(array, axis, 0, 0, tiled=True)


def on_device(hidden, queries, values, codes, exponents, base, momentum):
    x, c, z, y = (lax.axis_index(name) for name in ("x", "c", "zl", "y"))
    place = jnp.stack([c, z, y]).astype(jnp.int32)
    rows = codes.shape[1]

    delta, part = prep(codes[0], exponents[0], base)
    part_all = lax.all_gather(part, "y", axis=0, tiled=True)

    sent = exchange(delta, ("x", "c"))
    hidden_in, _ = lax.optimization_barrier((hidden[0], part))
    hidden_deal = deal([hidden_in], "zl")
    eighth = jnp.sum(sent.astype(jnp.float32), axis=0).astype(jnp.bfloat16)
    pair = add(eighth, swap(eighth, "zh", [(0, 1), (2, 3)])).astype(jnp.bfloat16)
    pair, *hidden_deal = lax.optimization_barrier((pair, *hidden_deal))
    mean = add(pair, swap(pair, "zh", [(1, 2), (3, 0)])) / (NX * NZH * NC)
    at = (x * NC + c) * BLOCK
    base_here = lax.dynamic_slice_in_dim(base, at, BLOCK, 1).astype(jnp.float32)
    moment_here = lax.dynamic_slice_in_dim(momentum, at, BLOCK, 1).astype(jnp.float32)
    moment_new = momentum_rate * moment_here + mean
    outer = (base_here - outer_rate * (mean + momentum_rate * moment_new)).astype(jnp.bfloat16)

    queries_in, values_in, outer = lax.optimization_barrier((queries[0], values[0], outer))
    both = jnp.stack(deal([queries_in, values_in], "zl"))

    same = gather(outer, ("x", "y"), NX * NY)
    other = lax.ppermute(same, "c", [(0, 1), (1, 0)])
    hidden_here, local = local_product(hidden_deal, part_all)
    other, both = lax.optimization_barrier((other, both))
    sums, own = project(place, hidden_here, local, same, other)

    value_all = lax.all_gather(both[:, :, 512:].reshape(512, KC // NZL), "y", axis=0)
    sums = exchange(sums, "zl")
    keys = (jnp.sum(sums.astype(jnp.float32), axis=0) / math.sqrt(D)).astype(jnp.bfloat16)
    mixed = attend(place, both, gather(keys, "y", NY), value_all)
    attended = jnp.transpose(exchange(mixed, "zl"), (1, 0, 2))

    whole = jnp.transpose(delta, (1, 0, 2)).reshape(rows, KC).astype(jnp.float32)
    blended = blend_share * (base.astype(jnp.float32) - whole) + (
        1.0 - blend_share
    ) * own.astype(jnp.float32)
    return blended.astype(jnp.bfloat16)[None], attended.reshape(1, 128, QH * HD)


def solution(mesh):
    split = Mesh(
        mesh.devices.reshape(NX, NZH, NC, NZL, NY),
        ("x", "zh", "c", "zl", "y"),
    )
    replica, fsdp = ("x", "zh", "c"), ("zl", "y")
    stacked = P(replica, fsdp, None)
    return jax.shard_map(
        on_device,
        mesh=split,
        in_specs=(stacked,) * 5 + (P(fsdp, None),) * 2,
        out_specs=(stacked, stacked),
        check_vma=False,
    )
```

```python
import math

import jax
import jax.numpy as jnp
from jax import lax
from jax.experimental import pallas as pl
from jax.experimental.pallas import tpu as pltpu
from jax.sharding import Mesh
from jax.sharding import PartitionSpec as P

D = 4608
HD = 128
QH = 16
KVH = 8
BLOCK = 128
KC = 1024
VMEM = pl.BlockSpec(memory_space=pltpu.VMEM)
SMEM = pl.BlockSpec(memory_space=pltpu.SMEM)

momentum_rate = 0.9
outer_rate = 0.7
blend_share = 0.25
logit_cap = 50.0
query_scalar = 12.0

NX, NZH, NC, NZL, NY = 4, 4, 2, 4, 4


def params(mib=40):
    return pltpu.CompilerParams(vmem_limit_bytes=mib << 20)


def prep_kernel(codes_ref, exps_ref, base_ref, delta_ref, part_ref):
    factor = jnp.exp2(exps_ref[...].astype(jnp.float32))
    for j in range(KC // BLOCK):
        cols = slice(j * BLOCK, (j + 1) * BLOCK)
        delta = codes_ref[:, cols].astype(jnp.float32) * factor[:, j : j + 1]
        delta_ref[j] = delta.astype(jnp.bfloat16)
        part_ref[:, cols] = (base_ref[:, cols].astype(jnp.float32) - delta).astype(jnp.bfloat16)


def prep(codes, exps, base):
    rows = codes.shape[0]
    return pl.pallas_call(
        prep_kernel,
        out_shape=(
            jax.ShapeDtypeStruct((KC // BLOCK, rows, BLOCK), jnp.bfloat16),
            jax.ShapeDtypeStruct((rows, KC), jnp.bfloat16),
        ),
        in_specs=[VMEM] * 3,
        out_specs=(VMEM, VMEM),
        compiler_params=params(),
        name="prep",
    )(codes, exps, base)


def local_kernel(h0_ref, h1_ref, h2_ref, h3_ref, part_ref, hidden_ref, out_ref):
    for s, ref in enumerate((h0_ref, h1_ref, h2_ref, h3_ref)):
        hidden_ref[s * 128 : (s + 1) * 128, :] = ref[...]
    for n in range(KC // 256):
        cols = slice(n * 256, (n + 1) * 256)
        out_ref[:, cols] = blend_share * jnp.dot(
            hidden_ref[...], part_ref[:, cols], preferred_element_type=jnp.float32
        )


def local_product(hidden, part):
    return pl.pallas_call(
        local_kernel,
        out_shape=(
            jax.ShapeDtypeStruct((512, part.shape[0]), jnp.bfloat16),
            jax.ShapeDtypeStruct((512, KC), jnp.float32),
        ),
        in_specs=[VMEM] * 5,
        out_specs=(VMEM, VMEM),
        compiler_params=params(),
        name="local_product",
    )(*hidden, part)


def project_kernel(place_ref, hidden_ref, local_ref, same_ref, other_ref, out_ref, own_ref, weight):
    rows = own_ref.shape[0]
    c, z, y = place_ref[0], place_ref[1], place_ref[2]
    for x in range(NX):
        for near, ref in enumerate((same_ref, other_ref)):
            at = (x * NC + lax.rem(c + near, NC)) * BLOCK
            cols = pl.ds(pl.multiple_of(at, BLOCK), BLOCK)
            own_ref[:, cols] = ref[x * NY + y]
            for ys in range(NY):
                weight[ys * rows : (ys + 1) * rows, cols] = ref[x * NY + ys]
    for n in range(NZL):
        cols = slice(n * 256, (n + 1) * 256)
        outer = jnp.dot(hidden_ref[...], weight[:, cols], preferred_element_type=jnp.float32)
        total = (local_ref[:, cols] + (1.0 - blend_share) * outer).astype(jnp.bfloat16)
        for s in range(NZL):
            at = pl.multiple_of(lax.rem(z - s + NZL, NZL) * 128, 128)
            out_ref[n, pl.ds(at, 128), :] = total[s * 128 : (s + 1) * 128]


def project(place, hidden, local, same, other):
    rows = same.shape[1]
    return pl.pallas_call(
        project_kernel,
        out_shape=(
            jax.ShapeDtypeStruct((NZL, 512, KC // NZL), jnp.bfloat16),
            jax.ShapeDtypeStruct((rows, KC), jnp.bfloat16),
        ),
        in_specs=[SMEM] + [VMEM] * 4,
        out_specs=(VMEM, VMEM),
        scratch_shapes=[pltpu.VMEM((NY * rows, KC), jnp.bfloat16)],
        compiler_params=params(),
        name="project",
    )(place, hidden, local, same, other)


def attend_kernel(place_ref, q_ref, keys, values, out_ref):
    z, y = place_ref[1], place_ref[2]
    row = lax.broadcasted_iota(jnp.int32, (256, 128), 0) % 128
    col = lax.broadcasted_iota(jnp.int32, (256, 128), 1)
    seen = col - row
    for zq in range(NZL):
        at = lax.rem(z - zq + NZL, NZL)
        q = jnp.concatenate([q_ref[at, :, :HD], q_ref[at, :, HD:]], axis=0)
        acc = jnp.zeros((256, HD), jnp.float32)
        total = jnp.zeros((256, 128), jnp.float32)
        for zk in range(zq + 1):
            rows = slice(zk * 128, (zk + 1) * 128)
            value_rows = pl.ds(pl.multiple_of(lax.rem(z - zk + NZL, NZL) * 128, 128), 128)
            for s in range(NY):
                scores = lax.dot_general(
                    q,
                    keys[s, rows, :],
                    (((1,), (1,)), ((), ())),
                    preferred_element_type=jnp.float32,
                )
                p = jnp.exp(logit_cap * jnp.tanh(scores * (1.0 / (query_scalar * logit_cap))))
                if zk == zq:
                    p = jnp.where(seen <= (y - s) * 128, p, 0.0)
                total += p
                acc += jnp.dot(
                    p.astype(jnp.bfloat16),
                    values[s, value_rows, :],
                    preferred_element_type=jnp.float32,
                )
        out = (acc / jnp.sum(total, axis=1, keepdims=True)).astype(jnp.bfloat16)
        out_ref[zq, :, :HD] = out[:128]
        out_ref[zq, :, HD:] = out[128:]


def attend(place, q, keys, values):
    kv_spec = pl.BlockSpec((NY, 512, HD), lambda h: (0, 0, h))
    q_spec = pl.BlockSpec((NZL, 128, 2 * HD), lambda h: (0, 0, h))
    return pl.pallas_call(
        attend_kernel,
        grid=(2,),
        out_shape=jax.ShapeDtypeStruct((NZL, 128, 4 * HD), jnp.bfloat16),
        in_specs=[SMEM, q_spec] + [kv_spec] * 2,
        out_specs=q_spec,
        compiler_params=params(),
        name="attend",
    )(place, q, keys, values)


def swap(array, axis, pairs):
    return lax.ppermute(array, axis, pairs + [(b, a) for a, b in pairs])


def add(a, b):
    return a.astype(jnp.float32) + b.astype(jnp.float32)


def deal(arrays, axis):
    at = lax.axis_index(axis)
    pieces = []
    for step in range(4):
        to = lax.rem(at + step, 4)
        cut = []
        for array in arrays:
            width = array.shape[1] // 4
            cut.append(lax.dynamic_slice_in_dim(array, to * width, width, 1))
        piece = jnp.concatenate(cut, axis=1)
        if step:
            piece = lax.ppermute(piece, axis, [(i, (i + step) % 4) for i in range(4)])
        pieces.append(piece)
    return pieces


def gather(array, axis, size):
    return lax.all_to_all(jnp.broadcast_to(array, (size,) + array.shape), axis, 0, 0, tiled=True)


def exchange(array, axis):
    return lax.all_to_all(array, axis, 0, 0, tiled=True)


def on_device(hidden, queries, values, codes, exponents, base, momentum):
    x, c, z, y = (lax.axis_index(name) for name in ("x", "c", "zl", "y"))
    place = jnp.stack([c, z, y]).astype(jnp.int32)
    rows = codes.shape[1]

    delta, part = prep(codes[0], exponents[0], base)
    part_all = lax.all_gather(part, "y", axis=0, tiled=True)

    sent = exchange(delta, ("x", "c"))
    hidden_deal = deal([hidden[0]], "zl")
    sent, *hidden_deal = lax.optimization_barrier((sent, *hidden_deal))
    eighth = jnp.sum(sent.astype(jnp.float32), axis=0).astype(jnp.bfloat16)
    pair = add(eighth, swap(eighth, "zh", [(0, 1), (2, 3)])).astype(jnp.bfloat16)
    mean = add(pair, swap(pair, "zh", [(1, 2), (3, 0)])) / (NX * NZH * NC)
    at = (x * NC + c) * BLOCK
    base_here = lax.dynamic_slice_in_dim(base, at, BLOCK, 1).astype(jnp.float32)
    moment_here = lax.dynamic_slice_in_dim(momentum, at, BLOCK, 1).astype(jnp.float32)
    moment_new = momentum_rate * moment_here + mean
    outer = (base_here - outer_rate * (mean + momentum_rate * moment_new)).astype(jnp.bfloat16)

    queries_in, values_in, outer = lax.optimization_barrier((queries[0], values[0], outer))
    both = jnp.stack(deal([queries_in, values_in], "zl"))

    same = gather(outer, ("x", "y"), NX * NY)
    hidden_here, local = local_product(hidden_deal, part_all)
    same, both, local = lax.optimization_barrier((same, both, local))
    other = lax.ppermute(same, "c", [(0, 1), (1, 0)])
    sums, own = project(place, hidden_here, local, same, other)

    value_all = lax.all_gather(both[:, :, 512:].reshape(512, KC // NZL), "y", axis=0)
    sums = exchange(sums, "zl")
    keys = (jnp.sum(sums.astype(jnp.float32), axis=0) / math.sqrt(D)).astype(jnp.bfloat16)
    mixed = attend(place, both, gather(keys, "y", NY), value_all)
    attended = jnp.transpose(exchange(mixed, "zl"), (1, 0, 2))

    whole = jnp.transpose(delta, (1, 0, 2)).reshape(rows, KC).astype(jnp.float32)
    blended = blend_share * (base.astype(jnp.float32) - whole) + (
        1.0 - blend_share
    ) * own.astype(jnp.float32)
    return blended.astype(jnp.bfloat16)[None], attended.reshape(1, 128, QH * HD)


def solution(mesh):
    split = Mesh(
        mesh.devices.reshape(NX, NZH, NC, NZL, NY),
        ("x", "zh", "c", "zl", "y"),
    )
    replica, fsdp = ("x", "zh", "c"), ("zl", "y")
    stacked = P(replica, fsdp, None)
    return jax.shard_map(
        on_device,
        mesh=split,
        in_specs=(stacked,) * 5 + (P(fsdp, None),) * 2,
        out_specs=(stacked, stacked),
        check_vma=False,
    )
```

```python
import math

import jax
import jax.numpy as jnp
from jax import lax
from jax.experimental import pallas as pl
from jax.experimental.pallas import tpu as pltpu
from jax.sharding import Mesh
from jax.sharding import PartitionSpec as P

D = 4608
HD = 128
QH = 16
KVH = 8
BLOCK = 128
KC = 1024
VMEM = pl.BlockSpec(memory_space=pltpu.VMEM)
SMEM = pl.BlockSpec(memory_space=pltpu.SMEM)
ANY = pl.BlockSpec(memory_space=pl.ANY)

momentum_rate = 0.9
outer_rate = 0.7
blend_share = 0.25
logit_cap = 50.0
query_scalar = 12.0

NX, NZH, NC, NZL, NY = 4, 4, 2, 4, 4


def params(mib=58):
    return pltpu.CompilerParams(vmem_limit_bytes=mib << 20)


def start_all(copies):
    for copy in copies:
        copy.start()
    return copies


def prep_kernel(codes_hbm, exps_ref, base_hbm, delta_ref, part_ref, codes, base, sems):
    half = codes.shape[0] // 2
    copies = []
    for i in range(2):
        rows = pl.ds(i * half, half)
        copies.append(pltpu.make_async_copy(codes_hbm.at[rows], codes.at[rows], sems.at[2 * i]))
        copies.append(pltpu.make_async_copy(base_hbm.at[rows], base.at[rows], sems.at[2 * i + 1]))
    start_all(copies)
    factor = jnp.exp2(exps_ref[...].astype(jnp.float32)).T
    for i in range(2):
        copies[2 * i].wait()
        copies[2 * i + 1].wait()
        rows = slice(i * half, (i + 1) * half)
        for j in range(KC // BLOCK):
            cols = slice(j * BLOCK, (j + 1) * BLOCK)
            delta = codes[rows, cols].astype(jnp.float32) * factor[rows, j : j + 1]
            delta_ref[j, rows] = delta.astype(jnp.bfloat16)
            part_ref[rows, cols] = (base[rows, cols].astype(jnp.float32) - delta).astype(
                jnp.bfloat16
            )


def prep(codes, exps, base):
    rows = codes.shape[0]
    return pl.pallas_call(
        prep_kernel,
        out_shape=(
            jax.ShapeDtypeStruct((KC // BLOCK, rows, BLOCK), jnp.bfloat16),
            jax.ShapeDtypeStruct((rows, KC), jnp.bfloat16),
        ),
        in_specs=[ANY, VMEM, ANY],
        out_specs=(VMEM, VMEM),
        scratch_shapes=[
            pltpu.VMEM((rows, KC), jnp.bfloat16),
            pltpu.VMEM((rows, KC), jnp.bfloat16),
            pltpu.SemaphoreType.DMA((4,)),
        ],
        compiler_params=params(),
        name="prep",
    )(codes, exps.T, base)


def step_kernel(place_ref, mine_ref, sent_ref, base_ref, momentum_ref, out_ref):
    mean = (mine_ref[...].astype(jnp.float32) + sent_ref[...].astype(jnp.float32)) * (
        1.0 / (NX * NZH * NC)
    )
    moment_new = momentum_rate * momentum_ref[...].astype(jnp.float32) + mean
    outer = base_ref[...].astype(jnp.float32) - outer_rate * (mean + momentum_rate * moment_new)
    outer = outer.astype(jnp.bfloat16)
    for i in range(out_ref.shape[0]):
        out_ref[i] = outer


def outer_step(place, mine, sent, base, momentum):
    rows = mine.shape[0]
    whole = pl.BlockSpec((rows, BLOCK), lambda i, p: (0, 0))
    block = pl.BlockSpec((rows, BLOCK), lambda i, p: (0, p[3]))
    return pl.pallas_call(
        step_kernel,
        out_shape=jax.ShapeDtypeStruct((NX * NY, rows, BLOCK), jnp.bfloat16),
        grid_spec=pltpu.PrefetchScalarGridSpec(
            num_scalar_prefetch=1,
            grid=(1,),
            in_specs=[whole, whole, block, block],
            out_specs=pl.BlockSpec((NX * NY, rows, BLOCK), lambda i, p: (0, 0, 0)),
        ),
        compiler_params=params(20),
        name="outer_step",
    )(place, mine, sent, base, momentum)


def project_kernel(place_ref, *refs):
    hidden_any, (part_any, same_any, other_any) = refs[:4], refs[4:7]
    out_ref, hidden, parts, outer, weight, part_sems, sems, hidden_sems = refs[7:]
    rows = outer.shape[1]
    c, z = place_ref[0], place_ref[1]
    part_copies, outer_copies, hidden_copies = [], [], []
    for n in range(NZL):
        cols = pl.ds(n * 2 * BLOCK, 2 * BLOCK)
        part_copies.append(
            pltpu.make_async_copy(part_any.at[:, cols], parts.at[n], part_sems.at[n])
        )
        for near, source in enumerate((same_any, other_any)):
            half = lax.rem(c + near, NC)
            at = pl.ds((n * NC + half) * NY, NY)
            outer_copies.append(
                pltpu.make_async_copy(
                    source.at[pl.ds(n * NY, NY)], outer.at[at], sems.at[n * NC + near]
                )
            )
    for s in range(NZL):
        to = pl.ds(pl.multiple_of(lax.rem(z - s + NZL, NZL) * 128, 128), 128)
        hidden_copies.append(
            pltpu.make_async_copy(hidden_any[s], hidden.at[to], hidden_sems.at[s])
        )
    start_all([part_copies[0]] + outer_copies[:2] + hidden_copies)
    for n in range(1, NZL):
        start_all([part_copies[n]] + outer_copies[2 * n : 2 * n + 2])
    for n in range(NZL):
        for copy in [part_copies[n]] + outer_copies[2 * n : 2 * n + 2]:
            copy.wait()
        for half in range(NC):
            cols = slice(half * BLOCK, (half + 1) * BLOCK)
            for y in range(NY):
                at = slice(y * rows, (y + 1) * rows)
                blend = blend_share * parts[n, at, cols].astype(jnp.float32)
                piece = outer[(n * NC + half) * NY + y].astype(jnp.float32)
                blend += (1.0 - blend_share) * piece
                weight[n, at, cols] = blend.astype(jnp.bfloat16)
        if n == 0:
            for copy in hidden_copies:
                copy.wait()
        keys = jnp.dot(hidden[...], weight[n], preferred_element_type=jnp.float32)
        out_ref[n] = keys.astype(jnp.bfloat16)


def project(place, hidden, part, same, other):
    rows = same.shape[1]
    depth = NY * rows
    return pl.pallas_call(
        project_kernel,
        out_shape=jax.ShapeDtypeStruct((NZL, 512, 2 * BLOCK), jnp.bfloat16),
        in_specs=[SMEM] + [ANY] * 7,
        out_specs=VMEM,
        scratch_shapes=[
            pltpu.VMEM((512, depth), jnp.bfloat16),
            pltpu.VMEM((NZL, depth, 2 * BLOCK), jnp.bfloat16),
            pltpu.VMEM((NZL * NC * NY, rows, BLOCK), jnp.bfloat16),
            pltpu.VMEM((NZL, depth, 2 * BLOCK), jnp.bfloat16),
            pltpu.SemaphoreType.DMA((NZL,)),
            pltpu.SemaphoreType.DMA((NZL * NC,)),
            pltpu.SemaphoreType.DMA((NZL,)),
        ],
        compiler_params=params(48),
        name="project",
    )(place, *hidden, part, same, other)


def reduce_kernel(sums_ref, out_ref):
    total = sums_ref[0].astype(jnp.float32)
    for i in range(1, NZL):
        total += sums_ref[i].astype(jnp.float32)
    keys = (total * (1.0 / math.sqrt(D))).astype(jnp.bfloat16)
    for i in range(NY):
        out_ref[i] = keys


def reduce_keys(sums):
    return pl.pallas_call(
        reduce_kernel,
        out_shape=jax.ShapeDtypeStruct((NY,) + sums.shape[1:], jnp.bfloat16),
        in_specs=[VMEM],
        out_specs=VMEM,
        compiler_params=params(20),
        name="reduce_keys",
    )(sums)


def blend_kernel(place_ref, delta_ref, base_ref, same_ref, other_ref, out_ref):
    c = place_ref[0]
    for x in range(NX):
        for near, ref in enumerate((same_ref, other_ref)):
            j = x * NC + lax.rem(c + near, NC)
            cols = pl.ds(pl.multiple_of(j * BLOCK, BLOCK), BLOCK)
            mine = base_ref[:, cols].astype(jnp.float32) - delta_ref[j].astype(jnp.float32)
            outer = ref[x, 0].astype(jnp.float32)
            blend = blend_share * mine + (1.0 - blend_share) * outer
            out_ref[:, cols] = blend.astype(jnp.bfloat16)


def blend(place, delta, base, same, other):
    rows = base.shape[0]
    piece = pl.BlockSpec((NX, 1, rows, BLOCK), lambda i, p: (0, p[2], 0, 0))
    split = (NX, NY, rows, BLOCK)
    return pl.pallas_call(
        blend_kernel,
        out_shape=jax.ShapeDtypeStruct((rows, KC), jnp.bfloat16),
        grid_spec=pltpu.PrefetchScalarGridSpec(
            num_scalar_prefetch=1,
            grid=(1,),
            in_specs=[
                pl.BlockSpec(delta.shape, lambda i, p: (0, 0, 0)),
                pl.BlockSpec((rows, KC), lambda i, p: (0, 0)),
                piece,
                piece,
            ],
            out_specs=pl.BlockSpec((rows, KC), lambda i, p: (0, 0)),
        ),
        compiler_params=params(20),
        name="blend",
    )(place, delta, base, same.reshape(split), other.reshape(split))


def attend_kernel(place_ref, *refs):
    pieces, keys_any, values_any = refs[:4], refs[4], refs[5:9]
    out_ref, queries, keys, values, query_sems, key_sems, value_sems = refs[9:]
    z, y = place_ref[1], place_ref[2]
    query_copies, key_copies, value_copies = [], [], []
    for s, ref in enumerate(pieces):
        at = lax.rem(z - s + NZL, NZL)
        query_copies.append(
            pltpu.make_async_copy(ref.at[:, pl.ds(0, 4 * HD)], queries.at[at], query_sems.at[s])
        )
    for zk in range(NZL):
        rows = pl.ds(zk * 128, 128)
        key_copies.append(
            pltpu.make_async_copy(keys_any.at[:, rows], keys.at[:, rows], key_sems.at[zk])
        )
        rows = pl.ds(pl.multiple_of(lax.rem(z - zk + NZL, NZL) * 128, 128), 128)
        for s in range(NY):
            value_copies.append(
                pltpu.make_async_copy(
                    values_any[s].at[rows],
                    values.at[zk, lax.rem(y - s + NY, NY)],
                    value_sems.at[zk, s],
                )
            )
    start_all(query_copies)
    for zk in range(NZL):
        start_all([key_copies[zk]] + value_copies[zk * NY : (zk + 1) * NY])
    row = lax.broadcasted_iota(jnp.int32, (256, 128), 0) % 128
    col = lax.broadcasted_iota(jnp.int32, (256, 128), 1)
    seen = col - row
    for copy in query_copies:
        copy.wait()
    for zq in range(NZL):
        for copy in [key_copies[zq]] + value_copies[zq * NY : (zq + 1) * NY]:
            copy.wait()
        for half in range(2):
            head = 2 * half * HD
            cols = slice(half * HD, (half + 1) * HD)
            q = jnp.concatenate(
                [queries[zq, :, head : head + HD], queries[zq, :, head + HD : head + 2 * HD]],
                axis=0,
            )
            acc = jnp.zeros((256, HD), jnp.float32)
            total = jnp.zeros((256, 128), jnp.float32)
            for zk in range(zq + 1):
                rows = slice(zk * 128, (zk + 1) * 128)
                for s in range(NY):
                    scores = lax.dot_general(
                        q,
                        keys[s, rows, cols],
                        (((1,), (1,)), ((), ())),
                        preferred_element_type=jnp.float32,
                    )
                    p = jnp.exp(
                        logit_cap * jnp.tanh(scores * (1.0 / (query_scalar * logit_cap)))
                    )
                    if zk == zq:
                        p = jnp.where(seen <= (y - s) * 128, p, 0.0)
                    total += p
                    acc += jnp.dot(
                        p.astype(jnp.bfloat16),
                        values[zk, s, :, cols],
                        preferred_element_type=jnp.float32,
                    )
            out = (acc / jnp.sum(total, axis=1, keepdims=True)).astype(jnp.bfloat16)
            out_ref[zq, :, head : head + HD] = out[:128]
            out_ref[zq, :, head + HD : head + 2 * HD] = out[128:]


def attend(place, queries, keys, values):
    return pl.pallas_call(
        attend_kernel,
        out_shape=jax.ShapeDtypeStruct((NZL, 128, 4 * HD), jnp.bfloat16),
        in_specs=[SMEM] + [ANY] * 9,
        out_specs=VMEM,
        scratch_shapes=[
            pltpu.VMEM((NZL, 128, 4 * HD), jnp.bfloat16),
            pltpu.VMEM((NY, 512, 2 * HD), jnp.bfloat16),
            pltpu.VMEM((NZL, NY, 128, 2 * HD), jnp.bfloat16),
            pltpu.SemaphoreType.DMA((NZL,)),
            pltpu.SemaphoreType.DMA((NZL,)),
            pltpu.SemaphoreType.DMA((NZL, NY)),
        ],
        compiler_params=params(20),
        name="attend",
    )(place, *queries, keys, *values)


def lay_kernel(mixed_any, out_any, sems):
    width = mixed_any.shape[2]
    copies = []
    for z in range(NZL):
        cols = pl.ds(z * width, width)
        copies.append(pltpu.make_async_copy(mixed_any.at[z], out_any.at[:, cols], sems.at[z]))
    for copy in start_all(copies):
        copy.wait()


def lay(mixed):
    places, rows, width = mixed.shape
    return pl.pallas_call(
        lay_kernel,
        out_shape=jax.ShapeDtypeStruct((rows, places * width), jnp.bfloat16),
        in_specs=[ANY],
        out_specs=ANY,
        scratch_shapes=[pltpu.SemaphoreType.DMA((NZL,))],
        compiler_params=params(20),
        name="lay",
    )(mixed)


def swap(array, axis, pairs):
    return lax.ppermute(array, axis, pairs + [(b, a) for a, b in pairs])


def add(a, b):
    return a.astype(jnp.float32) + b.astype(jnp.float32)


def deal(arrays, axis):
    at = lax.axis_index(axis)
    pieces = []
    for step in range(4):
        to = lax.rem(at + step, 4)
        cut = []
        for array in arrays:
            width = array.shape[1] // 4
            cut.append(lax.dynamic_slice_in_dim(array, to * width, width, 1))
        piece = jnp.concatenate(cut, axis=1)
        if step:
            piece = lax.ppermute(piece, axis, [(i, (i + step) % 4) for i in range(4)])
        pieces.append(piece)
    return pieces


def from_ring(array, axis):
    shifts = [[(i, (i + step) % 4) for i in range(4)] for step in (1, 2, 3)]
    return [array] + [lax.ppermute(array, axis, shift) for shift in shifts]


def exchange(array, axis):
    return lax.all_to_all(array, axis, 0, 0, tiled=True)


def on_device(hidden, queries, values, codes, exponents, base, momentum):
    x, c, z, y = (lax.axis_index(name) for name in ("x", "c", "zl", "y"))
    place = jnp.stack([c, z, y, x * NC + c]).astype(jnp.int32)

    delta, part = prep(codes[0], exponents[0], base)
    part_all = lax.all_gather(part, "y", axis=0, tiled=True)

    sent = exchange(delta, ("x", "c"))
    hidden_here = deal([hidden[0]], "zl")
    sent, hidden_here[1] = lax.optimization_barrier((sent, hidden_here[1]))
    eighth = jnp.sum(sent.astype(jnp.float32), axis=0).astype(jnp.bfloat16)
    pair = add(eighth, swap(eighth, "zh", [(0, 1), (2, 3)])).astype(jnp.bfloat16)
    swapped = swap(pair, "zh", [(1, 2), (3, 0)])
    swapped, hidden_here[2], hidden_here[3] = lax.optimization_barrier(
        (swapped, hidden_here[2], hidden_here[3])
    )
    outer = outer_step(place, pair, swapped, base, momentum)

    queries_in, values_in, outer = lax.optimization_barrier((queries[0], values[0], outer))
    both = deal([queries_in, values_in], "zl")

    same = exchange(outer, ("x", "y"))
    value_here = jnp.concatenate([piece[:, 512:] for piece in both])
    same, value_here, *both = lax.optimization_barrier((same, value_here, *both))
    other = lax.ppermute(same, "c", [(0, 1), (1, 0)])

    sums = project(place, hidden_here, part_all, same, other)
    sums, value_here = lax.optimization_barrier((sums, value_here))
    sums = exchange(sums, "zl")
    value_all = from_ring(value_here, "y")
    blended = blend(place, delta, base, same, other)
    sums, blended, *value_all = lax.optimization_barrier((sums, blended, *value_all))
    keys = exchange(reduce_keys(sums), "y")
    mixed = exchange(attend(place, both, keys, value_all), "zl")
    return blended[None], lay(mixed)[None]


def solution(mesh):
    split = Mesh(
        mesh.devices.reshape(NX, NZH, NC, NZL, NY),
        ("x", "zh", "c", "zl", "y"),
    )
    replica, fsdp = ("x", "zh", "c"), ("zl", "y")
    stacked = P(replica, fsdp, None)
    return jax.shard_map(
        on_device,
        mesh=split,
        in_specs=(stacked,) * 5 + (P(fsdp, None),) * 2,
        out_specs=(stacked, stacked),
        check_vma=False,
    )
```

```python
import math

import jax
import jax.numpy as jnp
from jax import lax
from jax.experimental import pallas as pl
from jax.experimental.pallas import tpu as pltpu
from jax.sharding import Mesh
from jax.sharding import PartitionSpec as P

D = 4608
HD = 128
QH = 16
KVH = 8
BLOCK = 128
KC = 1024
VMEM = pl.BlockSpec(memory_space=pltpu.VMEM)
SMEM = pl.BlockSpec(memory_space=pltpu.SMEM)
ANY = pl.BlockSpec(memory_space=pl.ANY)

momentum_rate = 0.9
outer_rate = 0.7
blend_share = 0.25
logit_cap = 50.0
query_scalar = 12.0

NX, NZH, NC, NZL, NY = 4, 4, 2, 4, 4


def params(mib=58):
    return pltpu.CompilerParams(vmem_limit_bytes=mib << 20)


def start_all(copies):
    for copy in copies:
        copy.start()
    return copies


def prep_kernel(codes_hbm, exps_ref, base_hbm, delta_ref, part_ref, codes, base, sems):
    half = codes.shape[0] // 2
    copies = []
    for i in range(2):
        rows = pl.ds(i * half, half)
        copies.append(pltpu.make_async_copy(codes_hbm.at[rows], codes.at[rows], sems.at[2 * i]))
        copies.append(pltpu.make_async_copy(base_hbm.at[rows], base.at[rows], sems.at[2 * i + 1]))
    start_all(copies)
    factor = jnp.exp2(exps_ref[...].astype(jnp.float32)).T
    for i in range(2):
        copies[2 * i].wait()
        copies[2 * i + 1].wait()
        rows = slice(i * half, (i + 1) * half)
        for j in range(KC // BLOCK):
            cols = slice(j * BLOCK, (j + 1) * BLOCK)
            delta = codes[rows, cols].astype(jnp.float32) * factor[rows, j : j + 1]
            delta_ref[j, rows] = delta.astype(jnp.bfloat16)
            part_ref[rows, cols] = (base[rows, cols].astype(jnp.float32) - delta).astype(
                jnp.bfloat16
            )


def prep(codes, exps, base):
    rows = codes.shape[0]
    return pl.pallas_call(
        prep_kernel,
        out_shape=(
            jax.ShapeDtypeStruct((KC // BLOCK, rows, BLOCK), jnp.bfloat16),
            jax.ShapeDtypeStruct((rows, KC), jnp.bfloat16),
        ),
        in_specs=[ANY, VMEM, ANY],
        out_specs=(VMEM, VMEM),
        scratch_shapes=[
            pltpu.VMEM((rows, KC), jnp.bfloat16),
            pltpu.VMEM((rows, KC), jnp.bfloat16),
            pltpu.SemaphoreType.DMA((4,)),
        ],
        compiler_params=params(),
        name="prep",
    )(codes, exps.T, base)


def step_kernel(place_ref, mine_ref, sent_ref, base_ref, momentum_ref, out_ref):
    mean = (mine_ref[...].astype(jnp.float32) + sent_ref[...].astype(jnp.float32)) * (
        1.0 / (NX * NZH * NC)
    )
    moment_new = momentum_rate * momentum_ref[...].astype(jnp.float32) + mean
    outer = base_ref[...].astype(jnp.float32) - outer_rate * (mean + momentum_rate * moment_new)
    outer = outer.astype(jnp.bfloat16)
    for i in range(out_ref.shape[0]):
        out_ref[i] = outer


def outer_step(place, mine, sent, base, momentum):
    rows = mine.shape[0]
    whole = pl.BlockSpec((rows, BLOCK), lambda i, p: (0, 0))
    block = pl.BlockSpec((rows, BLOCK), lambda i, p: (0, p[3]))
    return pl.pallas_call(
        step_kernel,
        out_shape=jax.ShapeDtypeStruct((NX * NY, rows, BLOCK), jnp.bfloat16),
        grid_spec=pltpu.PrefetchScalarGridSpec(
            num_scalar_prefetch=1,
            grid=(1,),
            in_specs=[whole, whole, block, block],
            out_specs=pl.BlockSpec((NX * NY, rows, BLOCK), lambda i, p: (0, 0, 0)),
        ),
        compiler_params=params(20),
        name="outer_step",
    )(place, mine, sent, base, momentum)


def project_kernel(place_ref, *refs):
    hidden_any, (part_any, same_any, other_any) = refs[:4], refs[4:7]
    out_ref, hidden, parts, outer, weight, part_sems, sems, hidden_sems = refs[7:]
    rows = outer.shape[1]
    c, z = place_ref[0], place_ref[1]
    part_copies, outer_copies, hidden_copies = [], [], []
    for n in range(NZL):
        cols = pl.ds(n * 2 * BLOCK, 2 * BLOCK)
        part_copies.append(
            pltpu.make_async_copy(part_any.at[:, cols], parts.at[n], part_sems.at[n])
        )
        for near, source in enumerate((same_any, other_any)):
            half = lax.rem(c + near, NC)
            at = pl.ds((n * NC + half) * NY, NY)
            outer_copies.append(
                pltpu.make_async_copy(
                    source.at[pl.ds(n * NY, NY)], outer.at[at], sems.at[n * NC + near]
                )
            )
    for s in range(NZL):
        to = pl.ds(pl.multiple_of(lax.rem(z - s + NZL, NZL) * 128, 128), 128)
        hidden_copies.append(
            pltpu.make_async_copy(hidden_any[s], hidden.at[to], hidden_sems.at[s])
        )
    start_all([part_copies[0]] + outer_copies[:2] + hidden_copies)
    for n in range(1, NZL):
        start_all([part_copies[n]] + outer_copies[2 * n : 2 * n + 2])
    for n in range(NZL):
        for copy in [part_copies[n]] + outer_copies[2 * n : 2 * n + 2]:
            copy.wait()
        for half in range(NC):
            cols = slice(half * BLOCK, (half + 1) * BLOCK)
            for y in range(NY):
                at = slice(y * rows, (y + 1) * rows)
                blend = blend_share * parts[n, at, cols].astype(jnp.float32)
                piece = outer[(n * NC + half) * NY + y].astype(jnp.float32)
                blend += (1.0 - blend_share) * piece
                weight[n, at, cols] = blend.astype(jnp.bfloat16)
        if n == 0:
            for copy in hidden_copies:
                copy.wait()
        keys = jnp.dot(hidden[...], weight[n], preferred_element_type=jnp.float32)
        out_ref[n] = keys.astype(jnp.bfloat16)


def project(place, hidden, part, same, other):
    rows = same.shape[1]
    depth = NY * rows
    return pl.pallas_call(
        project_kernel,
        out_shape=jax.ShapeDtypeStruct((NZL, 512, 2 * BLOCK), jnp.bfloat16),
        in_specs=[SMEM] + [ANY] * 7,
        out_specs=VMEM,
        scratch_shapes=[
            pltpu.VMEM((512, depth), jnp.bfloat16),
            pltpu.VMEM((NZL, depth, 2 * BLOCK), jnp.bfloat16),
            pltpu.VMEM((NZL * NC * NY, rows, BLOCK), jnp.bfloat16),
            pltpu.VMEM((NZL, depth, 2 * BLOCK), jnp.bfloat16),
            pltpu.SemaphoreType.DMA((NZL,)),
            pltpu.SemaphoreType.DMA((NZL * NC,)),
            pltpu.SemaphoreType.DMA((NZL,)),
        ],
        compiler_params=params(46),
        name="project",
    )(place, *hidden, part, same, other)


def reduce_kernel(sums_ref, out_ref):
    for head in range(2):
        cols = slice(head * HD, (head + 1) * HD)
        total = sums_ref[0, :, cols].astype(jnp.float32)
        for i in range(1, NZL):
            total += sums_ref[i, :, cols].astype(jnp.float32)
        keys = (total * (1.0 / math.sqrt(D))).astype(jnp.bfloat16)
        out_ref[2 * head] = keys
        out_ref[2 * head + 1] = keys


def reduce_keys(sums):
    return pl.pallas_call(
        reduce_kernel,
        out_shape=jax.ShapeDtypeStruct((NY, sums.shape[1], HD), jnp.bfloat16),
        in_specs=[VMEM],
        out_specs=VMEM,
        compiler_params=params(20),
        name="reduce_keys",
    )(sums)


def regroup_kernel(place_ref, *refs):
    pieces, outs, sems = refs[:4], refs[4:8], refs[8]
    z, y = place_ref[1], place_ref[2]
    copies = []
    for step in range(NY):
        to_y = lax.rem(y + step, NY)
        query_at = pl.multiple_of(to_y * HD, HD)
        value_at = pl.multiple_of(4 * HD + (to_y // 2) * HD, HD)
        for s in range(NZL):
            rows = pl.ds(pl.multiple_of(lax.rem(z - s + NZL, NZL) * 128, 128), 128)
            for i, at in enumerate((query_at, value_at)):
                copies.append(
                    pltpu.make_async_copy(
                        pieces[s].at[:, pl.ds(at, HD)],
                        outs[step].at[rows, pl.ds(i * HD, HD)],
                        sems.at[step, s, i],
                    )
                )
    for copy in start_all(copies):
        copy.wait()


def regroup(place, pieces):
    return pl.pallas_call(
        regroup_kernel,
        out_shape=[jax.ShapeDtypeStruct((512, 2 * HD), jnp.bfloat16)] * NY,
        in_specs=[SMEM] + [ANY] * 4,
        out_specs=[ANY] * NY,
        scratch_shapes=[pltpu.SemaphoreType.DMA((NY, NZL, 2))],
        compiler_params=params(20),
        name="regroup",
    )(place, *pieces)


def blend_kernel(place_ref, delta_ref, base_ref, same_ref, other_ref, out_ref):
    c = place_ref[0]
    for x in range(NX):
        for near, ref in enumerate((same_ref, other_ref)):
            j = x * NC + lax.rem(c + near, NC)
            cols = pl.ds(pl.multiple_of(j * BLOCK, BLOCK), BLOCK)
            mine = base_ref[:, cols].astype(jnp.float32) - delta_ref[j].astype(jnp.float32)
            outer = ref[x, 0].astype(jnp.float32)
            blend = blend_share * mine + (1.0 - blend_share) * outer
            out_ref[:, cols] = blend.astype(jnp.bfloat16)


def blend(place, delta, base, same, other):
    rows = base.shape[0]
    piece = pl.BlockSpec((NX, 1, rows, BLOCK), lambda i, p: (0, p[2], 0, 0))
    split = (NX, NY, rows, BLOCK)
    return pl.pallas_call(
        blend_kernel,
        out_shape=jax.ShapeDtypeStruct((rows, KC), jnp.bfloat16),
        grid_spec=pltpu.PrefetchScalarGridSpec(
            num_scalar_prefetch=1,
            grid=(1,),
            in_specs=[
                pl.BlockSpec(delta.shape, lambda i, p: (0, 0, 0)),
                pl.BlockSpec((rows, KC), lambda i, p: (0, 0)),
                piece,
                piece,
            ],
            out_specs=pl.BlockSpec((rows, KC), lambda i, p: (0, 0)),
        ),
        compiler_params=params(20),
        name="blend",
    )(place, delta, base, same.reshape(split), other.reshape(split))


def attend_kernel(place_ref, keys_any, *refs):
    pieces, (out_ref, queries, keys, values, sems) = refs[:4], refs[4:]
    y = place_ref[2]
    copies = [pltpu.make_async_copy(keys_any, keys, sems.at[0])]
    for i, target in enumerate((queries, values)):
        for s in range(NY):
            copies.append(
                pltpu.make_async_copy(
                    pieces[s].at[:, pl.ds(i * HD, HD)],
                    target.at[lax.rem(y - s + NY, NY)],
                    sems.at[1 + i * NY + s],
                )
            )
    start_all(copies)
    seen = lax.broadcasted_iota(jnp.int32, (256, 256), 1) <= lax.broadcasted_iota(
        jnp.int32, (256, 256), 0
    )
    for copy in copies:
        copy.wait()

    def pair(ref, z, at):
        return ref[2 * at : 2 * at + 2, z * 128 : (z + 1) * 128, :].reshape(256, HD)

    for at in range(2 * NZL):
        q = pair(queries, at // 2, at % 2)
        acc = jnp.zeros((256, HD), jnp.float32)
        total = jnp.zeros((256, 128), jnp.float32)
        for by in range(at + 1):
            scores = lax.dot_general(
                q,
                pair(keys, by // 2, by % 2),
                (((1,), (1,)), ((), ())),
                preferred_element_type=jnp.float32,
            )
            p = jnp.exp(logit_cap * jnp.tanh(scores * (1.0 / (query_scalar * logit_cap))))
            if by == at:
                p = jnp.where(seen, p, 0.0)
            total += p[:, :128] + p[:, 128:]
            acc += jnp.dot(
                p.astype(jnp.bfloat16),
                pair(values, by // 2, by % 2),
                preferred_element_type=jnp.float32,
            )
        out = (acc / jnp.sum(total, axis=1, keepdims=True)).astype(jnp.bfloat16)
        out_ref[2 * at] = out[:128]
        out_ref[2 * at + 1] = out[128:]


def attend(place, keys, pieces):
    whole = pltpu.VMEM((NY, 512, HD), jnp.bfloat16)
    return pl.pallas_call(
        attend_kernel,
        out_shape=jax.ShapeDtypeStruct((NZL * NY, 128, HD), jnp.bfloat16),
        in_specs=[SMEM] + [ANY] * 5,
        out_specs=VMEM,
        scratch_shapes=[whole, whole, whole, pltpu.SemaphoreType.DMA((1 + 2 * NY,))],
        compiler_params=params(20),
        name="attend",
    )(place, keys, *pieces)


def lay_kernel(mixed_any, out_any, sems):
    places, _, width = mixed_any.shape
    copies = []
    for i in range(places):
        cols = pl.ds(i * width, width)
        copies.append(pltpu.make_async_copy(mixed_any.at[i], out_any.at[:, cols], sems.at[i]))
    for copy in start_all(copies):
        copy.wait()


def lay(mixed):
    places, rows, width = mixed.shape
    return pl.pallas_call(
        lay_kernel,
        out_shape=jax.ShapeDtypeStruct((rows, places * width), jnp.bfloat16),
        in_specs=[ANY],
        out_specs=ANY,
        scratch_shapes=[pltpu.SemaphoreType.DMA((places,))],
        compiler_params=params(20),
        name="lay",
    )(mixed)


def swap(array, axis, pairs):
    return lax.ppermute(array, axis, pairs + [(b, a) for a, b in pairs])


def add(a, b):
    return a.astype(jnp.float32) + b.astype(jnp.float32)


def deal(arrays, axis):
    at = lax.axis_index(axis)
    pieces = []
    for step in range(4):
        to = lax.rem(at + step, 4)
        cut = []
        for array in arrays:
            width = array.shape[1] // 4
            cut.append(lax.dynamic_slice_in_dim(array, to * width, width, 1))
        piece = jnp.concatenate(cut, axis=1)
        if step:
            piece = lax.ppermute(piece, axis, [(i, (i + step) % 4) for i in range(4)])
        pieces.append(piece)
    return pieces


def turn(arrays, axis):
    shifts = [[(i, (i + step) % 4) for i in range(4)] for step in (1, 2, 3)]
    return arrays[:1] + [lax.ppermute(a, axis, shift) for a, shift in zip(arrays[1:], shifts)]


def exchange(array, axis):
    return lax.all_to_all(array, axis, 0, 0, tiled=True)


def on_device(hidden, queries, values, codes, exponents, base, momentum):
    x, c, z, y = (lax.axis_index(name) for name in ("x", "c", "zl", "y"))
    place = jnp.stack([c, z, y, x * NC + c]).astype(jnp.int32)

    delta, part = prep(codes[0], exponents[0], base)
    part_all = lax.all_gather(part, "y", axis=0, tiled=True)

    sent = exchange(delta, ("x", "c"))
    hidden_here = deal([hidden[0]], "zl")
    sent, hidden_here[2] = lax.optimization_barrier((sent, hidden_here[2]))
    eighth = jnp.sum(sent.astype(jnp.float32), axis=0).astype(jnp.bfloat16)
    pair = add(eighth, swap(eighth, "zh", [(0, 1), (2, 3)])).astype(jnp.bfloat16)
    swapped = swap(pair, "zh", [(1, 2), (3, 0)])
    swapped, hidden_here[1], hidden_here[3] = lax.optimization_barrier(
        (swapped, hidden_here[1], hidden_here[3])
    )
    outer = outer_step(place, pair, swapped, base, momentum)

    queries_in, values_in, outer = lax.optimization_barrier((queries[0], values[0], outer))
    both = deal([queries_in, values_in], "zl")

    same = exchange(outer, ("x", "y"))
    same, *both = lax.optimization_barrier((same, *both))
    other = lax.ppermute(same, "c", [(0, 1), (1, 0)])

    sums = project(place, hidden_here, part_all, same, other)
    sums, *both = lax.optimization_barrier((sums, *both))
    sums = exchange(sums, "zl")
    by_head = turn(list(regroup(place, both)), "y")
    blended = blend(place, delta, base, same, other)
    sums, blended, *by_head = lax.optimization_barrier((sums, blended, *by_head))
    keys = exchange(reduce_keys(sums), "y")
    mixed = exchange(attend(place, keys, by_head), ("zl", "y"))
    return blended[None], lay(mixed)[None]


def solution(mesh):
    split = Mesh(
        mesh.devices.reshape(NX, NZH, NC, NZL, NY),
        ("x", "zh", "c", "zl", "y"),
    )
    replica, fsdp = ("x", "zh", "c"), ("zl", "y")
    stacked = P(replica, fsdp, None)
    return jax.shard_map(
        on_device,
        mesh=split,
        in_specs=(stacked,) * 5 + (P(fsdp, None),) * 2,
        out_specs=(stacked, stacked),
        check_vma=False,
    )
```

```python
import math

import jax
import jax.numpy as jnp
from jax import lax
from jax.experimental import pallas as pl
from jax.experimental.pallas import tpu as pltpu
from jax.sharding import Mesh
from jax.sharding import PartitionSpec as P

D = 4608
HD = 128
QH = 16
KVH = 8
BLOCK = 128
KC = 1024
VMEM = pl.BlockSpec(memory_space=pltpu.VMEM)
SMEM = pl.BlockSpec(memory_space=pltpu.SMEM)
ANY = pl.BlockSpec(memory_space=pl.ANY)

momentum_rate = 0.9
outer_rate = 0.7
blend_share = 0.25
logit_cap = 50.0
query_scalar = 12.0

NX, NZH, NC, NZL, NY = 4, 4, 2, 4, 4


def params(mib=58):
    return pltpu.CompilerParams(vmem_limit_bytes=mib << 20)


def start_all(copies):
    for copy in copies:
        copy.start()
    return copies


def prep_kernel(codes_hbm, exps_ref, base_hbm, delta_ref, part_ref, codes, base, sems):
    half = codes.shape[0] // 2
    copies = []
    for i in range(2):
        rows = pl.ds(i * half, half)
        copies.append(pltpu.make_async_copy(codes_hbm.at[rows], codes.at[rows], sems.at[2 * i]))
        copies.append(pltpu.make_async_copy(base_hbm.at[rows], base.at[rows], sems.at[2 * i + 1]))
    start_all(copies)
    factor = jnp.exp2(exps_ref[...].astype(jnp.float32)).T
    for i in range(2):
        copies[2 * i].wait()
        copies[2 * i + 1].wait()
        rows = slice(i * half, (i + 1) * half)
        for j in range(KC // BLOCK):
            cols = slice(j * BLOCK, (j + 1) * BLOCK)
            delta = codes[rows, cols].astype(jnp.float32) * factor[rows, j : j + 1]
            delta_ref[j, rows] = delta.astype(jnp.bfloat16)
            part_ref[rows, cols] = (base[rows, cols].astype(jnp.float32) - delta).astype(
                jnp.bfloat16
            )


def prep(codes, exps, base):
    rows = codes.shape[0]
    return pl.pallas_call(
        prep_kernel,
        out_shape=(
            jax.ShapeDtypeStruct((KC // BLOCK, rows, BLOCK), jnp.bfloat16),
            jax.ShapeDtypeStruct((rows, KC), jnp.bfloat16),
        ),
        in_specs=[ANY, VMEM, ANY],
        out_specs=(VMEM, VMEM),
        scratch_shapes=[
            pltpu.VMEM((rows, KC), jnp.bfloat16),
            pltpu.VMEM((rows, KC), jnp.bfloat16),
            pltpu.SemaphoreType.DMA((4,)),
        ],
        compiler_params=params(),
        name="prep",
    )(codes, exps.T, base)


def step_kernel(place_ref, mine_ref, sent_ref, base_ref, momentum_ref, out_ref):
    mean = (mine_ref[...].astype(jnp.float32) + sent_ref[...].astype(jnp.float32)) * (
        1.0 / (NX * NZH * NC)
    )
    moment_new = momentum_rate * momentum_ref[...].astype(jnp.float32) + mean
    outer = base_ref[...].astype(jnp.float32) - outer_rate * (mean + momentum_rate * moment_new)
    outer = outer.astype(jnp.bfloat16)
    for i in range(out_ref.shape[0]):
        out_ref[i] = outer


def outer_step(place, mine, sent, base, momentum):
    rows = mine.shape[0]
    whole = pl.BlockSpec((rows, BLOCK), lambda i, p: (0, 0))
    block = pl.BlockSpec((rows, BLOCK), lambda i, p: (0, p[3]))
    return pl.pallas_call(
        step_kernel,
        out_shape=jax.ShapeDtypeStruct((NX * NY, rows, BLOCK), jnp.bfloat16),
        grid_spec=pltpu.PrefetchScalarGridSpec(
            num_scalar_prefetch=1,
            grid=(1,),
            in_specs=[whole, whole, block, block],
            out_specs=pl.BlockSpec((NX * NY, rows, BLOCK), lambda i, p: (0, 0, 0)),
        ),
        compiler_params=params(20),
        name="outer_step",
    )(place, mine, sent, base, momentum)


def project_kernel(place_ref, *refs):
    hidden_any, (part_any, same_any, other_any) = refs[:4], refs[4:7]
    out_ref, hidden, parts, outer, weight, part_sems, sems, hidden_sems = refs[7:]
    rows = outer.shape[1]
    c, z = place_ref[0], place_ref[1]
    part_copies, outer_copies, hidden_copies = [], [], []
    for n in range(NZL):
        cols = pl.ds(n * 2 * BLOCK, 2 * BLOCK)
        part_copies.append(
            pltpu.make_async_copy(part_any.at[:, cols], parts.at[n], part_sems.at[n])
        )
        for near, source in enumerate((same_any, other_any)):
            half = lax.rem(c + near, NC)
            at = pl.ds((n * NC + half) * NY, NY)
            outer_copies.append(
                pltpu.make_async_copy(
                    source.at[pl.ds(n * NY, NY)], outer.at[at], sems.at[n * NC + near]
                )
            )
    for s in range(NZL):
        to = pl.ds(pl.multiple_of(lax.rem(z - s + NZL, NZL) * 128, 128), 128)
        hidden_copies.append(
            pltpu.make_async_copy(hidden_any[s], hidden.at[to], hidden_sems.at[s])
        )
    start_all([part_copies[0]] + outer_copies[:2] + hidden_copies)
    for n in range(1, NZL):
        start_all([part_copies[n]] + outer_copies[2 * n : 2 * n + 2])
    for n in range(NZL):
        for copy in [part_copies[n]] + outer_copies[2 * n : 2 * n + 2]:
            copy.wait()
        for half in range(NC):
            cols = slice(half * BLOCK, (half + 1) * BLOCK)
            for y in range(NY):
                at = slice(y * rows, (y + 1) * rows)
                blend = blend_share * parts[n, at, cols].astype(jnp.float32)
                piece = outer[(n * NC + half) * NY + y].astype(jnp.float32)
                blend += (1.0 - blend_share) * piece
                weight[n, at, cols] = blend.astype(jnp.bfloat16)
        if n == 0:
            for copy in hidden_copies:
                copy.wait()
        keys = jnp.dot(hidden[...], weight[n], preferred_element_type=jnp.float32)
        out_ref[n] = keys.astype(jnp.bfloat16)


def project(place, hidden, part, same, other):
    rows = same.shape[1]
    depth = NY * rows
    return pl.pallas_call(
        project_kernel,
        out_shape=jax.ShapeDtypeStruct((NZL, 512, 2 * BLOCK), jnp.bfloat16),
        in_specs=[SMEM] + [ANY] * 7,
        out_specs=VMEM,
        scratch_shapes=[
            pltpu.VMEM((512, depth), jnp.bfloat16),
            pltpu.VMEM((NZL, depth, 2 * BLOCK), jnp.bfloat16),
            pltpu.VMEM((NZL * NC * NY, rows, BLOCK), jnp.bfloat16),
            pltpu.VMEM((NZL, depth, 2 * BLOCK), jnp.bfloat16),
            pltpu.SemaphoreType.DMA((NZL,)),
            pltpu.SemaphoreType.DMA((NZL * NC,)),
            pltpu.SemaphoreType.DMA((NZL,)),
        ],
        compiler_params=params(48),
        name="project",
    )(place, *hidden, part, same, other)


def reduce_kernel(sums_ref, out_ref):
    for head in range(2):
        cols = slice(head * HD, (head + 1) * HD)
        total = sums_ref[0, :, cols].astype(jnp.float32)
        for i in range(1, NZL):
            total += sums_ref[i, :, cols].astype(jnp.float32)
        keys = (total * (1.0 / math.sqrt(D))).astype(jnp.bfloat16)
        out_ref[2 * head] = keys
        out_ref[2 * head + 1] = keys


def reduce_keys(sums):
    return pl.pallas_call(
        reduce_kernel,
        out_shape=jax.ShapeDtypeStruct((NY, sums.shape[1], HD), jnp.bfloat16),
        in_specs=[VMEM],
        out_specs=VMEM,
        compiler_params=params(20),
        name="reduce_keys",
    )(sums)


def regroup_kernel(place_ref, *refs):
    pieces, outs, sems = refs[:4], refs[4:8], refs[8]
    z, y = place_ref[1], place_ref[2]
    copies = []
    for step in range(NY):
        to_y = lax.rem(y + step, NY)
        query_at = pl.multiple_of(to_y * HD, HD)
        value_at = pl.multiple_of(4 * HD + (to_y // 2) * HD, HD)
        for s in range(NZL):
            rows = pl.ds(pl.multiple_of(lax.rem(z - s + NZL, NZL) * 128, 128), 128)
            for i, at in enumerate((query_at, value_at)):
                copies.append(
                    pltpu.make_async_copy(
                        pieces[s].at[:, pl.ds(at, HD)],
                        outs[step].at[rows, pl.ds(i * HD, HD)],
                        sems.at[step, s, i],
                    )
                )
    for copy in start_all(copies):
        copy.wait()


def regroup(place, pieces):
    return pl.pallas_call(
        regroup_kernel,
        out_shape=[jax.ShapeDtypeStruct((512, 2 * HD), jnp.bfloat16)] * NY,
        in_specs=[SMEM] + [ANY] * 4,
        out_specs=[ANY] * NY,
        scratch_shapes=[pltpu.SemaphoreType.DMA((NY, NZL, 2))],
        compiler_params=params(20),
        name="regroup",
    )(place, *pieces)


def blend_kernel(place_ref, delta_ref, base_ref, same_ref, other_ref, out_ref):
    c = place_ref[0]
    for x in range(NX):
        for near, ref in enumerate((same_ref, other_ref)):
            j = x * NC + lax.rem(c + near, NC)
            cols = pl.ds(pl.multiple_of(j * BLOCK, BLOCK), BLOCK)
            mine = base_ref[:, cols].astype(jnp.float32) - delta_ref[j].astype(jnp.float32)
            outer = ref[x, 0].astype(jnp.float32)
            blend = blend_share * mine + (1.0 - blend_share) * outer
            out_ref[:, cols] = blend.astype(jnp.bfloat16)


def blend(place, delta, base, same, other):
    rows = base.shape[0]
    piece = pl.BlockSpec((NX, 1, rows, BLOCK), lambda i, p: (0, p[2], 0, 0))
    split = (NX, NY, rows, BLOCK)
    return pl.pallas_call(
        blend_kernel,
        out_shape=jax.ShapeDtypeStruct((rows, KC), jnp.bfloat16),
        grid_spec=pltpu.PrefetchScalarGridSpec(
            num_scalar_prefetch=1,
            grid=(1,),
            in_specs=[
                pl.BlockSpec(delta.shape, lambda i, p: (0, 0, 0)),
                pl.BlockSpec((rows, KC), lambda i, p: (0, 0)),
                piece,
                piece,
            ],
            out_specs=pl.BlockSpec((rows, KC), lambda i, p: (0, 0)),
        ),
        compiler_params=params(20),
        name="blend",
    )(place, delta, base, same.reshape(split), other.reshape(split))


def attend_kernel(place_ref, keys_any, *refs):
    pieces, (out_ref, queries, keys, values, sems) = refs[:4], refs[4:]
    y = place_ref[2]
    copies = [pltpu.make_async_copy(keys_any, keys, sems.at[0])]
    for i, target in enumerate((queries, values)):
        for s in range(NY):
            copies.append(
                pltpu.make_async_copy(
                    pieces[s].at[:, pl.ds(i * HD, HD)],
                    target.at[lax.rem(y - s + NY, NY)],
                    sems.at[1 + i * NY + s],
                )
            )
    start_all(copies)
    seen = lax.broadcasted_iota(jnp.int32, (256, 256), 1) <= lax.broadcasted_iota(
        jnp.int32, (256, 256), 0
    )
    for copy in copies:
        copy.wait()

    def pair(ref, z, at):
        return ref[2 * at : 2 * at + 2, z * 128 : (z + 1) * 128, :].reshape(256, HD)

    for at in range(2 * NZL):
        q = pair(queries, at // 2, at % 2)
        acc = jnp.zeros((256, HD), jnp.float32)
        total = jnp.zeros((256, 128), jnp.float32)
        for by in range(at + 1):
            scores = lax.dot_general(
                q,
                pair(keys, by // 2, by % 2),
                (((1,), (1,)), ((), ())),
                preferred_element_type=jnp.float32,
            )
            p = jnp.exp(logit_cap * jnp.tanh(scores * (1.0 / (query_scalar * logit_cap))))
            if by == at:
                p = jnp.where(seen, p, 0.0)
            total += p[:, :128] + p[:, 128:]
            acc += jnp.dot(
                p.astype(jnp.bfloat16),
                pair(values, by // 2, by % 2),
                preferred_element_type=jnp.float32,
            )
        out = (acc / jnp.sum(total, axis=1, keepdims=True)).astype(jnp.bfloat16)
        out_ref[2 * at] = out[:128]
        out_ref[2 * at + 1] = out[128:]


def attend(place, keys, pieces):
    whole = pltpu.VMEM((NY, 512, HD), jnp.bfloat16)
    return pl.pallas_call(
        attend_kernel,
        out_shape=jax.ShapeDtypeStruct((NZL * NY, 128, HD), jnp.bfloat16),
        in_specs=[SMEM] + [ANY] * 5,
        out_specs=VMEM,
        scratch_shapes=[whole, whole, whole, pltpu.SemaphoreType.DMA((1 + 2 * NY,))],
        compiler_params=params(20),
        name="attend",
    )(place, keys, *pieces)


def lay_kernel(mixed_any, out_any, sems):
    places, _, width = mixed_any.shape
    copies = []
    for i in range(places):
        cols = pl.ds(i * width, width)
        copies.append(pltpu.make_async_copy(mixed_any.at[i], out_any.at[:, cols], sems.at[i]))
    for copy in start_all(copies):
        copy.wait()


def lay(mixed):
    places, rows, width = mixed.shape
    return pl.pallas_call(
        lay_kernel,
        out_shape=jax.ShapeDtypeStruct((rows, places * width), jnp.bfloat16),
        in_specs=[ANY],
        out_specs=ANY,
        scratch_shapes=[pltpu.SemaphoreType.DMA((places,))],
        compiler_params=params(20),
        name="lay",
    )(mixed)


def swap(array, axis, pairs):
    return lax.ppermute(array, axis, pairs + [(b, a) for a, b in pairs])


def add(a, b):
    return a.astype(jnp.float32) + b.astype(jnp.float32)


def deal(arrays, axis):
    at = lax.axis_index(axis)
    pieces = []
    for step in range(4):
        to = lax.rem(at + step, 4)
        cut = []
        for array in arrays:
            width = array.shape[1] // 4
            cut.append(lax.dynamic_slice_in_dim(array, to * width, width, 1))
        piece = jnp.concatenate(cut, axis=1)
        if step:
            piece = lax.ppermute(piece, axis, [(i, (i + step) % 4) for i in range(4)])
        pieces.append(piece)
    return pieces


def turn(arrays, axis):
    shifts = [[(i, (i + step) % 4) for i in range(4)] for step in (1, 2, 3)]
    return arrays[:1] + [lax.ppermute(a, axis, shift) for a, shift in zip(arrays[1:], shifts)]


def exchange(array, axis):
    return lax.all_to_all(array, axis, 0, 0, tiled=True)


def on_device(hidden, queries, values, codes, exponents, base, momentum):
    x, c, z, y = (lax.axis_index(name) for name in ("x", "c", "zl", "y"))
    place = jnp.stack([c, z, y, x * NC + c]).astype(jnp.int32)

    delta, part = prep(codes[0], exponents[0], base)
    part_all = lax.all_gather(part, "y", axis=0, tiled=True)

    sent = exchange(delta, ("x", "c"))
    hidden_here = deal([hidden[0]], "zl")
    sent, hidden_here[1] = lax.optimization_barrier((sent, hidden_here[1]))
    eighth = jnp.sum(sent.astype(jnp.float32), axis=0).astype(jnp.bfloat16)
    pair = add(eighth, swap(eighth, "zh", [(0, 1), (2, 3)])).astype(jnp.bfloat16)
    swapped = swap(pair, "zh", [(1, 2), (3, 0)])
    both = deal([queries[0], values[0]], "zl")
    swapped, hidden_here[2], hidden_here[3], both[1], both[3] = lax.optimization_barrier(
        (swapped, hidden_here[2], hidden_here[3], both[1], both[3])
    )
    outer = outer_step(place, pair, swapped, base, momentum)

    same = exchange(outer, ("x", "y"))
    same, *both = lax.optimization_barrier((same, *both))
    other = lax.ppermute(same, "c", [(0, 1), (1, 0)])

    sums = project(place, hidden_here, part_all, same, other)
    sums, *both = lax.optimization_barrier((sums, *both))
    sums = exchange(sums, "zl")
    by_head = turn(list(regroup(place, both)), "y")
    blended = blend(place, delta, base, same, other)
    sums, blended, *by_head = lax.optimization_barrier((sums, blended, *by_head))
    keys = exchange(reduce_keys(sums), "y")
    mixed = exchange(attend(place, keys, by_head), ("zl", "y"))
    return blended[None], lay(mixed)[None]


def solution(mesh):
    split = Mesh(
        mesh.devices.reshape(NX, NZH, NC, NZL, NY),
        ("x", "zh", "c", "zl", "y"),
    )
    replica, fsdp = ("x", "zh", "c"), ("zl", "y")
    stacked = P(replica, fsdp, None)
    return jax.shard_map(
        on_device,
        mesh=split,
        in_specs=(stacked,) * 5 + (P(fsdp, None),) * 2,
        out_specs=(stacked, stacked),
        check_vma=False,
    )
```

```python
import math

import jax
import jax.numpy as jnp
from jax import lax
from jax.experimental import pallas as pl
from jax.experimental.pallas import tpu as pltpu
from jax.sharding import Mesh
from jax.sharding import PartitionSpec as P

D = 4608
HD = 128
QH = 16
KVH = 8
BLOCK = 128
KC = 1024
VMEM = pl.BlockSpec(memory_space=pltpu.VMEM)
SMEM = pl.BlockSpec(memory_space=pltpu.SMEM)
ANY = pl.BlockSpec(memory_space=pl.ANY)

momentum_rate = 0.9
outer_rate = 0.7
blend_share = 0.25
logit_cap = 50.0
query_scalar = 12.0

NX, NZH, NC, NZL, NY = 4, 4, 2, 4, 4


def params(mib=58):
    return pltpu.CompilerParams(vmem_limit_bytes=mib << 20)


def start_all(copies):
    for copy in copies:
        copy.start()
    return copies


def prep_kernel(codes_hbm, exps_ref, base_hbm, delta_ref, part_ref, codes, base, sems):
    half = codes.shape[0] // 2
    copies = []
    for i in range(2):
        rows = pl.ds(i * half, half)
        copies.append(pltpu.make_async_copy(codes_hbm.at[rows], codes.at[rows], sems.at[2 * i]))
        copies.append(pltpu.make_async_copy(base_hbm.at[rows], base.at[rows], sems.at[2 * i + 1]))
    start_all(copies)
    factor = jnp.exp2(exps_ref[...].astype(jnp.float32)).T
    for i in range(2):
        copies[2 * i].wait()
        copies[2 * i + 1].wait()
        rows = slice(i * half, (i + 1) * half)
        for j in range(KC // BLOCK):
            cols = slice(j * BLOCK, (j + 1) * BLOCK)
            delta = codes[rows, cols].astype(jnp.float32) * factor[rows, j : j + 1]
            delta_ref[j, rows] = delta.astype(jnp.bfloat16)
            part_ref[rows, cols] = (base[rows, cols].astype(jnp.float32) - delta).astype(
                jnp.bfloat16
            )


def prep(codes, exps, base):
    rows = codes.shape[0]
    return pl.pallas_call(
        prep_kernel,
        out_shape=(
            jax.ShapeDtypeStruct((KC // BLOCK, rows, BLOCK), jnp.bfloat16),
            jax.ShapeDtypeStruct((rows, KC), jnp.bfloat16),
        ),
        in_specs=[ANY, VMEM, ANY],
        out_specs=(VMEM, VMEM),
        scratch_shapes=[
            pltpu.VMEM((rows, KC), jnp.bfloat16),
            pltpu.VMEM((rows, KC), jnp.bfloat16),
            pltpu.SemaphoreType.DMA((4,)),
        ],
        compiler_params=params(),
        name="prep",
    )(codes, exps.T, base)


def step_kernel(place_ref, mine_ref, sent_ref, base_ref, momentum_ref, out_ref):
    mean = (mine_ref[...].astype(jnp.float32) + sent_ref[...].astype(jnp.float32)) * (
        1.0 / (NX * NZH * NC)
    )
    moment_new = momentum_rate * momentum_ref[...].astype(jnp.float32) + mean
    outer = base_ref[...].astype(jnp.float32) - outer_rate * (mean + momentum_rate * moment_new)
    outer = outer.astype(jnp.bfloat16)
    for i in range(out_ref.shape[0]):
        out_ref[i] = outer


def outer_step(place, mine, sent, base, momentum):
    rows = mine.shape[0]
    whole = pl.BlockSpec((rows, BLOCK), lambda i, p: (0, 0))
    block = pl.BlockSpec((rows, BLOCK), lambda i, p: (0, p[3]))
    return pl.pallas_call(
        step_kernel,
        out_shape=jax.ShapeDtypeStruct((NX * NY, rows, BLOCK), jnp.bfloat16),
        grid_spec=pltpu.PrefetchScalarGridSpec(
            num_scalar_prefetch=1,
            grid=(1,),
            in_specs=[whole, whole, block, block],
            out_specs=pl.BlockSpec((NX * NY, rows, BLOCK), lambda i, p: (0, 0, 0)),
        ),
        compiler_params=params(20),
        name="outer_step",
    )(place, mine, sent, base, momentum)


def local_kernel(place_ref, *refs):
    pieces, part_any, hidden_ref, out_ref, part, sems = refs[:4], *refs[4:]
    z = place_ref[1]
    copies = []
    for s in range(NZL):
        to = pl.ds(pl.multiple_of(lax.rem(z - s + NZL, NZL) * 128, 128), 128)
        copies.append(pltpu.make_async_copy(pieces[s], hidden_ref.at[to], sems.at[s]))
    for n in range(NZL):
        cols = pl.ds(n * 256, 256)
        copies.append(pltpu.make_async_copy(part_any.at[:, cols], part.at[n], sems.at[NZL + n]))
    start_all(copies)
    for copy in copies[:NZL]:
        copy.wait()
    for n in range(NZL):
        copies[NZL + n].wait()
        out_ref[n] = blend_share * jnp.dot(
            hidden_ref[...], part[n], preferred_element_type=jnp.float32
        )


def local_product(place, hidden, part):
    depth = part.shape[0]
    return pl.pallas_call(
        local_kernel,
        out_shape=(
            jax.ShapeDtypeStruct((512, depth), jnp.bfloat16),
            jax.ShapeDtypeStruct((NZL, 512, 256), jnp.float32),
        ),
        in_specs=[SMEM] + [ANY] * 5,
        out_specs=(VMEM, VMEM),
        scratch_shapes=[
            pltpu.VMEM((NZL, depth, 256), jnp.bfloat16),
            pltpu.SemaphoreType.DMA((2 * NZL,)),
        ],
        compiler_params=params(),
        name="local_product",
    )(place, *hidden, part)


def project_kernel(place_ref, hidden_any, local_any, same_any, other_any, out_ref, *refs):
    hidden, local, weight, sems, local_sems, hidden_sem = refs
    c = place_ref[0]
    hidden_copy = pltpu.make_async_copy(hidden_any, hidden, hidden_sem)
    copies = []
    for n in range(NZL):
        for near, source in enumerate((same_any, other_any)):
            at = pl.multiple_of(lax.rem(c + near, NC) * BLOCK, BLOCK)
            copies.append(
                pltpu.make_async_copy(
                    source.at[n], weight.at[n, :, pl.ds(at, BLOCK)], sems.at[n, near]
                )
            )
        copies.append(pltpu.make_async_copy(local_any.at[n], local.at[n], local_sems.at[n]))
    start_all(copies[:2] + [hidden_copy] + copies[2:])
    hidden_copy.wait()
    for n in range(NZL):
        for copy in copies[3 * n : 3 * n + 3]:
            copy.wait()
        outer = jnp.dot(hidden[...], weight[n], preferred_element_type=jnp.float32)
        out_ref[n] = (local[n] + (1.0 - blend_share) * outer).astype(jnp.bfloat16)


def project(place, hidden, local, same, other):
    depth = hidden.shape[1]
    blocks = (NZL, depth, BLOCK)
    return pl.pallas_call(
        project_kernel,
        out_shape=jax.ShapeDtypeStruct((NZL, 512, 2 * BLOCK), jnp.bfloat16),
        in_specs=[SMEM] + [ANY] * 4,
        out_specs=VMEM,
        scratch_shapes=[
            pltpu.VMEM((512, depth), jnp.bfloat16),
            pltpu.VMEM((NZL, 512, 256), jnp.float32),
            pltpu.VMEM((NZL, depth, 2 * BLOCK), jnp.bfloat16),
            pltpu.SemaphoreType.DMA((NZL, 2)),
            pltpu.SemaphoreType.DMA((NZL,)),
            pltpu.SemaphoreType.DMA,
        ],
        compiler_params=params(),
        name="project",
    )(place, hidden, local, same.reshape(blocks), other.reshape(blocks))


def reduce_kernel(sums_ref, out_ref):
    for head in range(2):
        cols = slice(head * HD, (head + 1) * HD)
        total = sums_ref[0, :, cols].astype(jnp.float32)
        for i in range(1, NZL):
            total += sums_ref[i, :, cols].astype(jnp.float32)
        keys = (total * (1.0 / math.sqrt(D))).astype(jnp.bfloat16)
        out_ref[2 * head] = keys
        out_ref[2 * head + 1] = keys


def reduce_keys(sums):
    return pl.pallas_call(
        reduce_kernel,
        out_shape=jax.ShapeDtypeStruct((NY, sums.shape[1], HD), jnp.bfloat16),
        in_specs=[VMEM],
        out_specs=VMEM,
        compiler_params=params(20),
        name="reduce_keys",
    )(sums)


def regroup_kernel(place_ref, *refs):
    pieces, outs, sems = refs[:4], refs[4:8], refs[8]
    z, y = place_ref[1], place_ref[2]
    copies = []
    for step in range(NY):
        to_y = lax.rem(y + step, NY)
        query_at = pl.multiple_of(to_y * HD, HD)
        value_at = pl.multiple_of(4 * HD + (to_y // 2) * HD, HD)
        for s in range(NZL):
            rows = pl.ds(pl.multiple_of(lax.rem(z - s + NZL, NZL) * 128, 128), 128)
            for i, at in enumerate((query_at, value_at)):
                copies.append(
                    pltpu.make_async_copy(
                        pieces[s].at[:, pl.ds(at, HD)],
                        outs[step].at[rows, pl.ds(i * HD, HD)],
                        sems.at[step, s, i],
                    )
                )
    for copy in start_all(copies):
        copy.wait()


def regroup(place, pieces):
    return pl.pallas_call(
        regroup_kernel,
        out_shape=[jax.ShapeDtypeStruct((512, 2 * HD), jnp.bfloat16)] * NY,
        in_specs=[SMEM] + [ANY] * 4,
        out_specs=[ANY] * NY,
        scratch_shapes=[pltpu.SemaphoreType.DMA((NY, NZL, 2))],
        compiler_params=params(20),
        name="regroup",
    )(place, *pieces)


def blend_kernel(place_ref, delta_ref, base_ref, same_ref, other_ref, out_ref):
    c = place_ref[0]
    for x in range(NX):
        for near, ref in enumerate((same_ref, other_ref)):
            j = x * NC + lax.rem(c + near, NC)
            cols = pl.ds(pl.multiple_of(j * BLOCK, BLOCK), BLOCK)
            mine = base_ref[:, cols].astype(jnp.float32) - delta_ref[j].astype(jnp.float32)
            outer = ref[x, 0].astype(jnp.float32)
            blend = blend_share * mine + (1.0 - blend_share) * outer
            out_ref[:, cols] = blend.astype(jnp.bfloat16)


def blend(place, delta, base, same, other):
    rows = base.shape[0]
    piece = pl.BlockSpec((NX, 1, rows, BLOCK), lambda i, p: (0, p[2], 0, 0))
    split = (NX, NY, rows, BLOCK)
    return pl.pallas_call(
        blend_kernel,
        out_shape=jax.ShapeDtypeStruct((rows, KC), jnp.bfloat16),
        grid_spec=pltpu.PrefetchScalarGridSpec(
            num_scalar_prefetch=1,
            grid=(1,),
            in_specs=[
                pl.BlockSpec(delta.shape, lambda i, p: (0, 0, 0)),
                pl.BlockSpec((rows, KC), lambda i, p: (0, 0)),
                piece,
                piece,
            ],
            out_specs=pl.BlockSpec((rows, KC), lambda i, p: (0, 0)),
        ),
        compiler_params=params(20),
        name="blend",
    )(place, delta, base, same.reshape(split), other.reshape(split))


def attend_kernel(place_ref, keys_any, *refs):
    pieces, (out_ref, queries, keys, values, sems) = refs[:4], refs[4:]
    y = place_ref[2]
    copies = [pltpu.make_async_copy(keys_any, keys, sems.at[0])]
    for i, target in enumerate((queries, values)):
        for s in range(NY):
            copies.append(
                pltpu.make_async_copy(
                    pieces[s].at[:, pl.ds(i * HD, HD)],
                    target.at[lax.rem(y - s + NY, NY)],
                    sems.at[1 + i * NY + s],
                )
            )
    start_all(copies)
    seen = lax.broadcasted_iota(jnp.int32, (256, 256), 1) <= lax.broadcasted_iota(
        jnp.int32, (256, 256), 0
    )
    for copy in copies:
        copy.wait()

    def pair(ref, z, at):
        return ref[2 * at : 2 * at + 2, z * 128 : (z + 1) * 128, :].reshape(256, HD)

    for at in range(2 * NZL):
        q = pair(queries, at // 2, at % 2)
        acc = jnp.zeros((256, HD), jnp.float32)
        total = jnp.zeros((256, 128), jnp.float32)
        for by in range(at + 1):
            scores = lax.dot_general(
                q,
                pair(keys, by // 2, by % 2),
                (((1,), (1,)), ((), ())),
                preferred_element_type=jnp.float32,
            )
            p = jnp.exp(logit_cap * jnp.tanh(scores * (1.0 / (query_scalar * logit_cap))))
            if by == at:
                p = jnp.where(seen, p, 0.0)
            total += p[:, :128] + p[:, 128:]
            acc += jnp.dot(
                p.astype(jnp.bfloat16),
                pair(values, by // 2, by % 2),
                preferred_element_type=jnp.float32,
            )
        out = (acc / jnp.sum(total, axis=1, keepdims=True)).astype(jnp.bfloat16)
        out_ref[2 * at] = out[:128]
        out_ref[2 * at + 1] = out[128:]


def attend(place, keys, pieces):
    whole = pltpu.VMEM((NY, 512, HD), jnp.bfloat16)
    return pl.pallas_call(
        attend_kernel,
        out_shape=jax.ShapeDtypeStruct((NZL * NY, 128, HD), jnp.bfloat16),
        in_specs=[SMEM] + [ANY] * 5,
        out_specs=VMEM,
        scratch_shapes=[whole, whole, whole, pltpu.SemaphoreType.DMA((1 + 2 * NY,))],
        compiler_params=params(20),
        name="attend",
    )(place, keys, *pieces)


def lay_kernel(mixed_any, out_any, sems):
    places, _, width = mixed_any.shape
    copies = []
    for i in range(places):
        cols = pl.ds(i * width, width)
        copies.append(pltpu.make_async_copy(mixed_any.at[i], out_any.at[:, cols], sems.at[i]))
    for copy in start_all(copies):
        copy.wait()


def lay(mixed):
    places, rows, width = mixed.shape
    return pl.pallas_call(
        lay_kernel,
        out_shape=jax.ShapeDtypeStruct((rows, places * width), jnp.bfloat16),
        in_specs=[ANY],
        out_specs=ANY,
        scratch_shapes=[pltpu.SemaphoreType.DMA((places,))],
        compiler_params=params(20),
        name="lay",
    )(mixed)


def swap(array, axis, pairs):
    return lax.ppermute(array, axis, pairs + [(b, a) for a, b in pairs])


def add(a, b):
    return a.astype(jnp.float32) + b.astype(jnp.float32)


def deal(arrays, axis):
    at = lax.axis_index(axis)
    pieces = []
    for step in range(4):
        to = lax.rem(at + step, 4)
        cut = []
        for array in arrays:
            width = array.shape[1] // 4
            cut.append(lax.dynamic_slice_in_dim(array, to * width, width, 1))
        piece = jnp.concatenate(cut, axis=1)
        if step:
            piece = lax.ppermute(piece, axis, [(i, (i + step) % 4) for i in range(4)])
        pieces.append(piece)
    return pieces


def turn(arrays, axis):
    shifts = [[(i, (i + step) % 4) for i in range(4)] for step in (1, 2, 3)]
    return arrays[:1] + [lax.ppermute(a, axis, shift) for a, shift in zip(arrays[1:], shifts)]


def exchange(array, axis):
    return lax.all_to_all(array, axis, 0, 0, tiled=True)


def on_device(hidden, queries, values, codes, exponents, base, momentum):
    x, c, z, y = (lax.axis_index(name) for name in ("x", "c", "zl", "y"))
    place = jnp.stack([c, z, y, x * NC + c]).astype(jnp.int32)

    delta, part = prep(codes[0], exponents[0], base)
    part_all = lax.all_gather(part, "y", axis=0, tiled=True)

    sent = exchange(delta, ("x", "c"))
    hidden_here = deal([hidden[0]], "zl")
    sent, hidden_here[1] = lax.optimization_barrier((sent, hidden_here[1]))
    eighth = jnp.sum(sent.astype(jnp.float32), axis=0).astype(jnp.bfloat16)
    pair = add(eighth, swap(eighth, "zh", [(0, 1), (2, 3)])).astype(jnp.bfloat16)
    pair, hidden_here[2] = lax.optimization_barrier((pair, hidden_here[2]))
    swapped = swap(pair, "zh", [(1, 2), (3, 0)])
    both = deal([queries[0], values[0]], "zl")
    swapped, hidden_here[3], both[1], both[3] = lax.optimization_barrier(
        (swapped, hidden_here[3], both[1], both[3])
    )
    outer = outer_step(place, pair, swapped, base, momentum)

    same = exchange(outer, ("x", "y"))
    ordered, local = local_product(place, hidden_here, part_all)
    same, ordered, local, *both = lax.optimization_barrier((same, ordered, local, *both))
    other = lax.ppermute(same, "c", [(0, 1), (1, 0)])

    sums = project(place, ordered, local, same, other)
    sums, *both = lax.optimization_barrier((sums, *both))
    sums = exchange(sums, "zl")
    by_head = turn(list(regroup(place, both)), "y")
    blended = blend(place, delta, base, same, other)
    sums, blended, *by_head = lax.optimization_barrier((sums, blended, *by_head))
    keys = exchange(reduce_keys(sums), "y")
    mixed = exchange(attend(place, keys, by_head), ("zl", "y"))
    return blended[None], lay(mixed)[None]


def solution(mesh):
    split = Mesh(
        mesh.devices.reshape(NX, NZH, NC, NZL, NY),
        ("x", "zh", "c", "zl", "y"),
    )
    replica, fsdp = ("x", "zh", "c"), ("zl", "y")
    stacked = P(replica, fsdp, None)
    return jax.shard_map(
        on_device,
        mesh=split,
        in_specs=(stacked,) * 5 + (P(fsdp, None),) * 2,
        out_specs=(stacked, stacked),
        check_vma=False,
    )
```

```python
import math

import jax
import jax.numpy as jnp
from jax import lax
from jax.experimental import pallas as pl
from jax.experimental.pallas import tpu as pltpu
from jax.sharding import Mesh
from jax.sharding import PartitionSpec as P

D = 4608
HD = 128
QH = 16
KVH = 8
BLOCK = 128
KC = 1024
VMEM = pl.BlockSpec(memory_space=pltpu.VMEM)
SMEM = pl.BlockSpec(memory_space=pltpu.SMEM)
ANY = pl.BlockSpec(memory_space=pl.ANY)

momentum_rate = 0.9
outer_rate = 0.7
blend_share = 0.25
logit_cap = 50.0
query_scalar = 12.0

NX, NZH, NC, NZL, NY = 4, 4, 2, 4, 4


def params(mib=58):
    return pltpu.CompilerParams(vmem_limit_bytes=mib << 20)


def start_all(copies):
    for copy in copies:
        copy.start()
    return copies


def prep_kernel(codes_hbm, exps_ref, base_hbm, delta_ref, part_ref, codes, base, sems):
    half = codes.shape[0] // 2
    copies = []
    for i in range(2):
        rows = pl.ds(i * half, half)
        copies.append(pltpu.make_async_copy(codes_hbm.at[rows], codes.at[rows], sems.at[2 * i]))
        copies.append(pltpu.make_async_copy(base_hbm.at[rows], base.at[rows], sems.at[2 * i + 1]))
    start_all(copies)
    factor = jnp.exp2(exps_ref[...].astype(jnp.float32)).T
    for i in range(2):
        copies[2 * i].wait()
        copies[2 * i + 1].wait()
        rows = slice(i * half, (i + 1) * half)
        for j in range(KC // BLOCK):
            cols = slice(j * BLOCK, (j + 1) * BLOCK)
            delta = codes[rows, cols].astype(jnp.float32) * factor[rows, j : j + 1]
            delta_ref[j, rows] = delta.astype(jnp.bfloat16)
            part_ref[rows, cols] = (base[rows, cols].astype(jnp.float32) - delta).astype(
                jnp.bfloat16
            )


def prep(codes, exps, base):
    rows = codes.shape[0]
    return pl.pallas_call(
        prep_kernel,
        out_shape=(
            jax.ShapeDtypeStruct((KC // BLOCK, rows, BLOCK), jnp.bfloat16),
            jax.ShapeDtypeStruct((rows, KC), jnp.bfloat16),
        ),
        in_specs=[ANY, VMEM, ANY],
        out_specs=(VMEM, VMEM),
        scratch_shapes=[
            pltpu.VMEM((rows, KC), jnp.bfloat16),
            pltpu.VMEM((rows, KC), jnp.bfloat16),
            pltpu.SemaphoreType.DMA((4,)),
        ],
        compiler_params=params(),
        name="prep",
    )(codes, exps.T, base)


def step_kernel(place_ref, mine_ref, sent_ref, base_ref, momentum_ref, out_ref):
    mean = (mine_ref[...].astype(jnp.float32) + sent_ref[...].astype(jnp.float32)) * (
        1.0 / (NX * NZH * NC)
    )
    moment_new = momentum_rate * momentum_ref[...].astype(jnp.float32) + mean
    outer = base_ref[...].astype(jnp.float32) - outer_rate * (mean + momentum_rate * moment_new)
    outer = outer.astype(jnp.bfloat16)
    for i in range(out_ref.shape[0]):
        out_ref[i] = outer


def outer_step(place, mine, sent, base, momentum):
    rows = mine.shape[0]
    whole = pl.BlockSpec((rows, BLOCK), lambda i, p: (0, 0))
    block = pl.BlockSpec((rows, BLOCK), lambda i, p: (0, p[3]))
    return pl.pallas_call(
        step_kernel,
        out_shape=jax.ShapeDtypeStruct((NX * NY, rows, BLOCK), jnp.bfloat16),
        grid_spec=pltpu.PrefetchScalarGridSpec(
            num_scalar_prefetch=1,
            grid=(1,),
            in_specs=[whole, whole, block, block],
            out_specs=pl.BlockSpec((NX * NY, rows, BLOCK), lambda i, p: (0, 0, 0)),
        ),
        compiler_params=params(20),
        name="outer_step",
    )(place, mine, sent, base, momentum)


def local_kernel(place_ref, *refs):
    pieces, part_any, hidden_ref, out_ref, part, sems = refs[:4], *refs[4:]
    z = place_ref[1]
    copies = []
    for s in range(NZL):
        to = pl.ds(pl.multiple_of(lax.rem(z - s + NZL, NZL) * 128, 128), 128)
        copies.append(pltpu.make_async_copy(pieces[s], hidden_ref.at[to], sems.at[s]))
    step = part.shape[0] // NY
    for y in range(NY):
        rows = pl.ds(y * step, step)
        copies.append(pltpu.make_async_copy(part_any.at[rows], part.at[rows], sems.at[NZL + y]))
    for copy in start_all(copies):
        copy.wait()
    for n in range(NZL):
        cols = slice(n * 256, (n + 1) * 256)
        out_ref[n] = blend_share * jnp.dot(
            hidden_ref[...], part[:, cols], preferred_element_type=jnp.float32
        )


def local_product(place, hidden, part):
    depth = part.shape[0]
    return pl.pallas_call(
        local_kernel,
        out_shape=(
            jax.ShapeDtypeStruct((512, depth), jnp.bfloat16),
            jax.ShapeDtypeStruct((NZL, 512, 256), jnp.float32),
        ),
        in_specs=[SMEM] + [ANY] * 5,
        out_specs=(VMEM, VMEM),
        scratch_shapes=[
            pltpu.VMEM(part.shape, jnp.bfloat16),
            pltpu.SemaphoreType.DMA((2 * NZL,)),
        ],
        compiler_params=params(48),
        name="local_product",
    )(place, *hidden, part)


def project_kernel(place_ref, hidden_ref, local_ref, same_ref, other_ref, out_ref, weight):
    c = place_ref[0]
    for n in range(NZL):
        for near, ref in enumerate((same_ref, other_ref)):
            at = pl.multiple_of(lax.rem(c + near, NC) * BLOCK, BLOCK)
            weight[n, :, pl.ds(at, BLOCK)] = ref[n]
        outer = jnp.dot(hidden_ref[...], weight[n], preferred_element_type=jnp.float32)
        out_ref[n] = (local_ref[n] + (1.0 - blend_share) * outer).astype(jnp.bfloat16)


def project(place, hidden, local, same, other):
    depth = hidden.shape[1]
    blocks = (NZL, depth, BLOCK)
    return pl.pallas_call(
        project_kernel,
        out_shape=jax.ShapeDtypeStruct((NZL, 512, 2 * BLOCK), jnp.bfloat16),
        in_specs=[SMEM] + [VMEM] * 4,
        out_specs=VMEM,
        scratch_shapes=[pltpu.VMEM((NZL, depth, 2 * BLOCK), jnp.bfloat16)],
        compiler_params=params(20),
        name="project",
    )(place, hidden, local, same.reshape(blocks), other.reshape(blocks))


def reduce_kernel(sums_ref, out_ref):
    for head in range(2):
        cols = slice(head * HD, (head + 1) * HD)
        total = sums_ref[0, :, cols].astype(jnp.float32)
        for i in range(1, NZL):
            total += sums_ref[i, :, cols].astype(jnp.float32)
        keys = (total * (1.0 / math.sqrt(D))).astype(jnp.bfloat16)
        out_ref[2 * head] = keys
        out_ref[2 * head + 1] = keys


def reduce_keys(sums):
    return pl.pallas_call(
        reduce_kernel,
        out_shape=jax.ShapeDtypeStruct((NY, sums.shape[1], HD), jnp.bfloat16),
        in_specs=[VMEM],
        out_specs=VMEM,
        compiler_params=params(20),
        name="reduce_keys",
    )(sums)


def regroup_kernel(place_ref, *refs):
    pieces, outs, sems = refs[:4], refs[4:8], refs[8]
    z, y = place_ref[1], place_ref[2]
    copies = []
    for step in range(NY):
        to_y = lax.rem(y + step, NY)
        query_at = pl.multiple_of(to_y * HD, HD)
        value_at = pl.multiple_of(4 * HD + (to_y // 2) * HD, HD)
        for s in range(NZL):
            rows = pl.ds(pl.multiple_of(lax.rem(z - s + NZL, NZL) * 128, 128), 128)
            for i, at in enumerate((query_at, value_at)):
                copies.append(
                    pltpu.make_async_copy(
                        pieces[s].at[:, pl.ds(at, HD)],
                        outs[step].at[rows, pl.ds(i * HD, HD)],
                        sems.at[step, s, i],
                    )
                )
    for copy in start_all(copies):
        copy.wait()


def regroup(place, pieces):
    return pl.pallas_call(
        regroup_kernel,
        out_shape=[jax.ShapeDtypeStruct((512, 2 * HD), jnp.bfloat16)] * NY,
        in_specs=[SMEM] + [ANY] * 4,
        out_specs=[ANY] * NY,
        scratch_shapes=[pltpu.SemaphoreType.DMA((NY, NZL, 2))],
        compiler_params=params(20),
        name="regroup",
    )(place, *pieces)


def blend_kernel(place_ref, delta_ref, base_ref, same_ref, other_ref, out_ref):
    c = place_ref[0]
    for x in range(NX):
        for near, ref in enumerate((same_ref, other_ref)):
            j = x * NC + lax.rem(c + near, NC)
            cols = pl.ds(pl.multiple_of(j * BLOCK, BLOCK), BLOCK)
            mine = base_ref[:, cols].astype(jnp.float32) - delta_ref[j].astype(jnp.float32)
            outer = ref[x, 0].astype(jnp.float32)
            blend = blend_share * mine + (1.0 - blend_share) * outer
            out_ref[:, cols] = blend.astype(jnp.bfloat16)


def blend(place, delta, base, same, other):
    rows = base.shape[0]
    piece = pl.BlockSpec((NX, 1, rows, BLOCK), lambda i, p: (0, p[2], 0, 0))
    split = (NX, NY, rows, BLOCK)
    return pl.pallas_call(
        blend_kernel,
        out_shape=jax.ShapeDtypeStruct((rows, KC), jnp.bfloat16),
        grid_spec=pltpu.PrefetchScalarGridSpec(
            num_scalar_prefetch=1,
            grid=(1,),
            in_specs=[
                pl.BlockSpec(delta.shape, lambda i, p: (0, 0, 0)),
                pl.BlockSpec((rows, KC), lambda i, p: (0, 0)),
                piece,
                piece,
            ],
            out_specs=pl.BlockSpec((rows, KC), lambda i, p: (0, 0)),
        ),
        compiler_params=params(20),
        name="blend",
    )(place, delta, base, same.reshape(split), other.reshape(split))


def attend_kernel(place_ref, keys_any, *refs):
    pieces, (out_ref, queries, keys, values, sems) = refs[:4], refs[4:]
    y = place_ref[2]
    copies = [pltpu.make_async_copy(keys_any, keys, sems.at[0])]
    for i, target in enumerate((queries, values)):
        for s in range(NY):
            copies.append(
                pltpu.make_async_copy(
                    pieces[s].at[:, pl.ds(i * HD, HD)],
                    target.at[lax.rem(y - s + NY, NY)],
                    sems.at[1 + i * NY + s],
                )
            )
    start_all(copies)
    seen = lax.broadcasted_iota(jnp.int32, (256, 256), 1) <= lax.broadcasted_iota(
        jnp.int32, (256, 256), 0
    )
    for copy in copies:
        copy.wait()

    def pair(ref, z, at):
        return ref[2 * at : 2 * at + 2, z * 128 : (z + 1) * 128, :].reshape(256, HD)

    for at in range(2 * NZL):
        q = pair(queries, at // 2, at % 2)
        acc = jnp.zeros((256, HD), jnp.float32)
        total = jnp.zeros((256, 128), jnp.float32)
        for by in range(at + 1):
            scores = lax.dot_general(
                q,
                pair(keys, by // 2, by % 2),
                (((1,), (1,)), ((), ())),
                preferred_element_type=jnp.float32,
            )
            p = jnp.exp(logit_cap * jnp.tanh(scores * (1.0 / (query_scalar * logit_cap))))
            if by == at:
                p = jnp.where(seen, p, 0.0)
            total += p[:, :128] + p[:, 128:]
            acc += jnp.dot(
                p.astype(jnp.bfloat16),
                pair(values, by // 2, by % 2),
                preferred_element_type=jnp.float32,
            )
        out = (acc / jnp.sum(total, axis=1, keepdims=True)).astype(jnp.bfloat16)
        out_ref[2 * at] = out[:128]
        out_ref[2 * at + 1] = out[128:]


def attend(place, keys, pieces):
    whole = pltpu.VMEM((NY, 512, HD), jnp.bfloat16)
    return pl.pallas_call(
        attend_kernel,
        out_shape=jax.ShapeDtypeStruct((NZL * NY, 128, HD), jnp.bfloat16),
        in_specs=[SMEM] + [ANY] * 5,
        out_specs=VMEM,
        scratch_shapes=[whole, whole, whole, pltpu.SemaphoreType.DMA((1 + 2 * NY,))],
        compiler_params=params(20),
        name="attend",
    )(place, keys, *pieces)


def lay_kernel(mixed_any, out_any, sems):
    places, _, width = mixed_any.shape
    copies = []
    for i in range(places):
        cols = pl.ds(i * width, width)
        copies.append(pltpu.make_async_copy(mixed_any.at[i], out_any.at[:, cols], sems.at[i]))
    for copy in start_all(copies):
        copy.wait()


def lay(mixed):
    places, rows, width = mixed.shape
    return pl.pallas_call(
        lay_kernel,
        out_shape=jax.ShapeDtypeStruct((rows, places * width), jnp.bfloat16),
        in_specs=[ANY],
        out_specs=ANY,
        scratch_shapes=[pltpu.SemaphoreType.DMA((places,))],
        compiler_params=params(20),
        name="lay",
    )(mixed)


def swap(array, axis, pairs):
    return lax.ppermute(array, axis, pairs + [(b, a) for a, b in pairs])


def add(a, b):
    return a.astype(jnp.float32) + b.astype(jnp.float32)


def deal(arrays, axis):
    at = lax.axis_index(axis)
    pieces = []
    for step in range(4):
        to = lax.rem(at + step, 4)
        cut = []
        for array in arrays:
            width = array.shape[1] // 4
            cut.append(lax.dynamic_slice_in_dim(array, to * width, width, 1))
        piece = jnp.concatenate(cut, axis=1)
        if step:
            piece = lax.ppermute(piece, axis, [(i, (i + step) % 4) for i in range(4)])
        pieces.append(piece)
    return pieces


def turn(arrays, axis):
    shifts = [[(i, (i + step) % 4) for i in range(4)] for step in (1, 2, 3)]
    return arrays[:1] + [lax.ppermute(a, axis, shift) for a, shift in zip(arrays[1:], shifts)]


def exchange(array, axis):
    return lax.all_to_all(array, axis, 0, 0, tiled=True)


def on_device(hidden, queries, values, codes, exponents, base, momentum):
    x, c, z, y = (lax.axis_index(name) for name in ("x", "c", "zl", "y"))
    place = jnp.stack([c, z, y, x * NC + c]).astype(jnp.int32)

    delta, part = prep(codes[0], exponents[0], base)
    part_all = lax.all_gather(part, "y", axis=0, tiled=True)

    sent = exchange(delta, ("x", "c"))
    hidden_here = deal([hidden[0]], "zl")
    sent, hidden_here[1] = lax.optimization_barrier((sent, hidden_here[1]))
    eighth = jnp.sum(sent.astype(jnp.float32), axis=0).astype(jnp.bfloat16)
    pair = add(eighth, swap(eighth, "zh", [(0, 1), (2, 3)])).astype(jnp.bfloat16)
    pair, hidden_here[2] = lax.optimization_barrier((pair, hidden_here[2]))
    swapped = swap(pair, "zh", [(1, 2), (3, 0)])
    both = deal([queries[0], values[0]], "zl")
    swapped, hidden_here[3], both[1], both[3] = lax.optimization_barrier(
        (swapped, hidden_here[3], both[1], both[3])
    )
    outer = outer_step(place, pair, swapped, base, momentum)

    same = exchange(outer, ("x", "y"))
    ordered, local = local_product(place, hidden_here, part_all)
    same, ordered, local, *both = lax.optimization_barrier((same, ordered, local, *both))
    other = lax.ppermute(same, "c", [(0, 1), (1, 0)])

    sums = project(place, ordered, local, same, other)
    sums, *both = lax.optimization_barrier((sums, *both))
    sums = exchange(sums, "zl")
    by_head = turn(list(regroup(place, both)), "y")
    blended = blend(place, delta, base, same, other)
    sums, blended, *by_head = lax.optimization_barrier((sums, blended, *by_head))
    keys = exchange(reduce_keys(sums), "y")
    mixed = exchange(attend(place, keys, by_head), ("zl", "y"))
    return blended[None], lay(mixed)[None]


def solution(mesh):
    split = Mesh(
        mesh.devices.reshape(NX, NZH, NC, NZL, NY),
        ("x", "zh", "c", "zl", "y"),
    )
    replica, fsdp = ("x", "zh", "c"), ("zl", "y")
    stacked = P(replica, fsdp, None)
    return jax.shard_map(
        on_device,
        mesh=split,
        in_specs=(stacked,) * 5 + (P(fsdp, None),) * 2,
        out_specs=(stacked, stacked),
        check_vma=False,
    )
```

```python
import math

import jax
import jax.numpy as jnp
from jax import lax
from jax.experimental import pallas as pl
from jax.experimental.pallas import tpu as pltpu
from jax.sharding import Mesh
from jax.sharding import PartitionSpec as P

D = 4608
HD = 128
QH = 16
KVH = 8
BLOCK = 128
KC = 1024
VMEM = pl.BlockSpec(memory_space=pltpu.VMEM)
SMEM = pl.BlockSpec(memory_space=pltpu.SMEM)
ANY = pl.BlockSpec(memory_space=pl.ANY)

momentum_rate = 0.9
outer_rate = 0.7
blend_share = 0.25
logit_cap = 50.0
query_scalar = 12.0

NX, NZH, NC, NZL, NY = 4, 4, 2, 4, 4


def params(mib=58):
    return pltpu.CompilerParams(vmem_limit_bytes=mib << 20)


def start_all(copies):
    for copy in copies:
        copy.start()
    return copies


def prep_kernel(codes_hbm, exps_ref, base_hbm, delta_ref, part_ref, codes, base, sems):
    half = codes.shape[0] // 2
    copies = []
    for i in range(2):
        rows = pl.ds(i * half, half)
        copies.append(pltpu.make_async_copy(codes_hbm.at[rows], codes.at[rows], sems.at[2 * i]))
        copies.append(pltpu.make_async_copy(base_hbm.at[rows], base.at[rows], sems.at[2 * i + 1]))
    start_all(copies)
    factor = jnp.exp2(exps_ref[...].astype(jnp.float32)).T
    for i in range(2):
        copies[2 * i].wait()
        copies[2 * i + 1].wait()
        rows = slice(i * half, (i + 1) * half)
        for j in range(KC // BLOCK):
            cols = slice(j * BLOCK, (j + 1) * BLOCK)
            delta = codes[rows, cols].astype(jnp.float32) * factor[rows, j : j + 1]
            delta_ref[j, rows] = delta.astype(jnp.bfloat16)
            part_ref[rows, cols] = (base[rows, cols].astype(jnp.float32) - delta).astype(
                jnp.bfloat16
            )


def prep(codes, exps, base):
    rows = codes.shape[0]
    return pl.pallas_call(
        prep_kernel,
        out_shape=(
            jax.ShapeDtypeStruct((KC // BLOCK, rows, BLOCK), jnp.bfloat16),
            jax.ShapeDtypeStruct((rows, KC), jnp.bfloat16),
        ),
        in_specs=[ANY, VMEM, ANY],
        out_specs=(VMEM, VMEM),
        scratch_shapes=[
            pltpu.VMEM((rows, KC), jnp.bfloat16),
            pltpu.VMEM((rows, KC), jnp.bfloat16),
            pltpu.SemaphoreType.DMA((4,)),
        ],
        compiler_params=params(),
        name="prep",
    )(codes, exps.T, base)


def step_kernel(place_ref, mine_ref, sent_ref, base_ref, momentum_ref, out_ref):
    mean = (mine_ref[...].astype(jnp.float32) + sent_ref[...].astype(jnp.float32)) * (
        1.0 / (NX * NZH * NC)
    )
    moment_new = momentum_rate * momentum_ref[...].astype(jnp.float32) + mean
    outer = base_ref[...].astype(jnp.float32) - outer_rate * (mean + momentum_rate * moment_new)
    outer = outer.astype(jnp.bfloat16)
    for i in range(out_ref.shape[0]):
        out_ref[i] = outer


def outer_step(place, mine, sent, base, momentum):
    rows = mine.shape[0]
    whole = pl.BlockSpec((rows, BLOCK), lambda i, p: (0, 0))
    block = pl.BlockSpec((rows, BLOCK), lambda i, p: (0, p[3]))
    return pl.pallas_call(
        step_kernel,
        out_shape=jax.ShapeDtypeStruct((NX * NY, rows, BLOCK), jnp.bfloat16),
        grid_spec=pltpu.PrefetchScalarGridSpec(
            num_scalar_prefetch=1,
            grid=(1,),
            in_specs=[whole, whole, block, block],
            out_specs=pl.BlockSpec((NX * NY, rows, BLOCK), lambda i, p: (0, 0, 0)),
        ),
        compiler_params=params(20),
        name="outer_step",
    )(place, mine, sent, base, momentum)


def local_kernel(place_ref, *refs):
    pieces, part_any, hidden_ref, out_ref, part, sems = refs[:4], *refs[4:]
    z = place_ref[1]
    copies = []
    for s in range(NZL):
        to = pl.ds(pl.multiple_of(lax.rem(z - s + NZL, NZL) * 128, 128), 128)
        copies.append(pltpu.make_async_copy(pieces[s], hidden_ref.at[to], sems.at[s]))
    step = part.shape[0] // NY
    for y in range(NY):
        rows = pl.ds(y * step, step)
        copies.append(pltpu.make_async_copy(part_any.at[rows], part.at[rows], sems.at[NZL + y]))
    for copy in start_all(copies):
        copy.wait()
    for n in range(NZL):
        cols = slice(n * 256, (n + 1) * 256)
        out_ref[n] = blend_share * jnp.dot(
            hidden_ref[...], part[:, cols], preferred_element_type=jnp.float32
        )


def local_product(place, hidden, part):
    depth = part.shape[0]
    return pl.pallas_call(
        local_kernel,
        out_shape=(
            jax.ShapeDtypeStruct((512, depth), jnp.bfloat16),
            jax.ShapeDtypeStruct((NZL, 512, 256), jnp.float32),
        ),
        in_specs=[SMEM] + [ANY] * 5,
        out_specs=(VMEM, VMEM),
        scratch_shapes=[
            pltpu.VMEM(part.shape, jnp.bfloat16),
            pltpu.SemaphoreType.DMA((2 * NZL,)),
        ],
        compiler_params=params(48),
        name="local_product",
    )(place, *hidden, part)


def project_kernel(place_ref, hidden_ref, local_ref, same_ref, other_ref, out_ref, weight):
    c = place_ref[0]
    for n in range(NZL):
        for near, ref in enumerate((same_ref, other_ref)):
            at = pl.multiple_of(lax.rem(c + near, NC) * BLOCK, BLOCK)
            weight[n, :, pl.ds(at, BLOCK)] = ref[n]
        outer = jnp.dot(hidden_ref[...], weight[n], preferred_element_type=jnp.float32)
        out_ref[n] = (local_ref[n] + (1.0 - blend_share) * outer).astype(jnp.bfloat16)


def project(place, hidden, local, same, other):
    depth = hidden.shape[1]
    blocks = (NZL, depth, BLOCK)
    return pl.pallas_call(
        project_kernel,
        out_shape=jax.ShapeDtypeStruct((NZL, 512, 2 * BLOCK), jnp.bfloat16),
        in_specs=[SMEM] + [VMEM] * 4,
        out_specs=VMEM,
        scratch_shapes=[pltpu.VMEM((NZL, depth, 2 * BLOCK), jnp.bfloat16)],
        compiler_params=params(20),
        name="project",
    )(place, hidden, local, same.reshape(blocks), other.reshape(blocks))


def reduce_kernel(sums_ref, out_ref):
    for head in range(2):
        cols = slice(head * HD, (head + 1) * HD)
        total = sums_ref[0, :, cols].astype(jnp.float32)
        for i in range(1, NZL):
            total += sums_ref[i, :, cols].astype(jnp.float32)
        keys = (total * (1.0 / math.sqrt(D))).astype(jnp.bfloat16)
        out_ref[2 * head] = keys
        out_ref[2 * head + 1] = keys


def reduce_keys(sums):
    return pl.pallas_call(
        reduce_kernel,
        out_shape=jax.ShapeDtypeStruct((NY, sums.shape[1], HD), jnp.bfloat16),
        in_specs=[VMEM],
        out_specs=VMEM,
        compiler_params=params(20),
        name="reduce_keys",
    )(sums)


def regroup_kernel(place_ref, *refs):
    pieces, outs, sems = refs[:4], refs[4:8], refs[8]
    z, y = place_ref[1], place_ref[2]
    copies = []
    for step in range(NY):
        to_y = lax.rem(y + step, NY)
        query_at = pl.multiple_of(to_y * HD, HD)
        value_at = pl.multiple_of(4 * HD + (to_y // 2) * HD, HD)
        for s in range(NZL):
            rows = pl.ds(pl.multiple_of(lax.rem(z - s + NZL, NZL) * 128, 128), 128)
            for i, at in enumerate((query_at, value_at)):
                copies.append(
                    pltpu.make_async_copy(
                        pieces[s].at[:, pl.ds(at, HD)],
                        outs[step].at[rows, pl.ds(i * HD, HD)],
                        sems.at[step, s, i],
                    )
                )
    for copy in start_all(copies):
        copy.wait()


def regroup(place, pieces):
    return pl.pallas_call(
        regroup_kernel,
        out_shape=[jax.ShapeDtypeStruct((512, 2 * HD), jnp.bfloat16)] * NY,
        in_specs=[SMEM] + [ANY] * 4,
        out_specs=[ANY] * NY,
        scratch_shapes=[pltpu.SemaphoreType.DMA((NY, NZL, 2))],
        compiler_params=params(20),
        name="regroup",
    )(place, *pieces)


def blend_kernel(place_ref, delta_ref, base_ref, same_ref, other_ref, out_ref):
    c = place_ref[0]
    for x in range(NX):
        for near, ref in enumerate((same_ref, other_ref)):
            j = x * NC + lax.rem(c + near, NC)
            cols = pl.ds(pl.multiple_of(j * BLOCK, BLOCK), BLOCK)
            mine = base_ref[:, cols].astype(jnp.float32) - delta_ref[j].astype(jnp.float32)
            outer = ref[x, 0].astype(jnp.float32)
            blend = blend_share * mine + (1.0 - blend_share) * outer
            out_ref[:, cols] = blend.astype(jnp.bfloat16)


def blend(place, delta, base, same, other):
    rows = base.shape[0]
    piece = pl.BlockSpec((NX, 1, rows, BLOCK), lambda i, p: (0, p[2], 0, 0))
    split = (NX, NY, rows, BLOCK)
    return pl.pallas_call(
        blend_kernel,
        out_shape=jax.ShapeDtypeStruct((rows, KC), jnp.bfloat16),
        grid_spec=pltpu.PrefetchScalarGridSpec(
            num_scalar_prefetch=1,
            grid=(1,),
            in_specs=[
                pl.BlockSpec(delta.shape, lambda i, p: (0, 0, 0)),
                pl.BlockSpec((rows, KC), lambda i, p: (0, 0)),
                piece,
                piece,
            ],
            out_specs=pl.BlockSpec((rows, KC), lambda i, p: (0, 0)),
        ),
        compiler_params=params(20),
        name="blend",
    )(place, delta, base, same.reshape(split), other.reshape(split))


def attend_kernel(place_ref, keys_any, *refs):
    pieces, (out_ref, queries, keys, values, sems) = refs[:4], refs[4:]
    y = place_ref[2]
    copies = [pltpu.make_async_copy(keys_any, keys, sems.at[0])]
    for i, target in enumerate((queries, values)):
        for s in range(NY):
            copies.append(
                pltpu.make_async_copy(
                    pieces[s].at[:, pl.ds(i * HD, HD)],
                    target.at[lax.rem(y - s + NY, NY)],
                    sems.at[1 + i * NY + s],
                )
            )
    start_all(copies)
    seen = lax.broadcasted_iota(jnp.int32, (256, 256), 1) <= lax.broadcasted_iota(
        jnp.int32, (256, 256), 0
    )
    for copy in copies:
        copy.wait()

    def pair(ref, z, at):
        return ref[2 * at : 2 * at + 2, z * 128 : (z + 1) * 128, :].reshape(256, HD)

    for at in range(2 * NZL):
        q = pair(queries, at // 2, at % 2)
        acc = jnp.zeros((256, HD), jnp.float32)
        total = jnp.zeros((256, 128), jnp.float32)
        for by in range(at + 1):
            scores = lax.dot_general(
                q,
                pair(keys, by // 2, by % 2),
                (((1,), (1,)), ((), ())),
                preferred_element_type=jnp.float32,
            )
            p = jnp.exp(logit_cap * jnp.tanh(scores * (1.0 / (query_scalar * logit_cap))))
            if by == at:
                p = jnp.where(seen, p, 0.0)
            total += p[:, :128] + p[:, 128:]
            acc += jnp.dot(
                p.astype(jnp.bfloat16),
                pair(values, by // 2, by % 2),
                preferred_element_type=jnp.float32,
            )
        out = (acc / jnp.sum(total, axis=1, keepdims=True)).astype(jnp.bfloat16)
        out_ref[2 * at] = out[:128]
        out_ref[2 * at + 1] = out[128:]


def attend(place, keys, pieces):
    whole = pltpu.VMEM((NY, 512, HD), jnp.bfloat16)
    return pl.pallas_call(
        attend_kernel,
        out_shape=jax.ShapeDtypeStruct((NZL * NY, 128, HD), jnp.bfloat16),
        in_specs=[SMEM] + [ANY] * 5,
        out_specs=VMEM,
        scratch_shapes=[whole, whole, whole, pltpu.SemaphoreType.DMA((1 + 2 * NY,))],
        compiler_params=params(20),
        name="attend",
    )(place, keys, *pieces)


def lay_kernel(mixed_any, out_any, sems):
    places, _, width = mixed_any.shape
    copies = []
    for i in range(places):
        cols = pl.ds(i * width, width)
        copies.append(pltpu.make_async_copy(mixed_any.at[i], out_any.at[:, cols], sems.at[i]))
    for copy in start_all(copies):
        copy.wait()


def lay(mixed):
    places, rows, width = mixed.shape
    return pl.pallas_call(
        lay_kernel,
        out_shape=jax.ShapeDtypeStruct((rows, places * width), jnp.bfloat16),
        in_specs=[ANY],
        out_specs=ANY,
        scratch_shapes=[pltpu.SemaphoreType.DMA((places,))],
        compiler_params=params(20),
        name="lay",
    )(mixed)


def swap(array, axis, pairs):
    return lax.ppermute(array, axis, pairs + [(b, a) for a, b in pairs])


def add(a, b):
    return a.astype(jnp.float32) + b.astype(jnp.float32)


def deal(arrays, axis):
    at = lax.axis_index(axis)
    pieces = []
    for step in range(4):
        to = lax.rem(at + step, 4)
        cut = []
        for array in arrays:
            width = array.shape[1] // 4
            cut.append(lax.dynamic_slice_in_dim(array, to * width, width, 1))
        piece = jnp.concatenate(cut, axis=1)
        if step:
            piece = lax.ppermute(piece, axis, [(i, (i + step) % 4) for i in range(4)])
        pieces.append(piece)
    return pieces


def turn(arrays, axis):
    shifts = [[(i, (i + step) % 4) for i in range(4)] for step in (1, 2, 3)]
    return arrays[:1] + [lax.ppermute(a, axis, shift) for a, shift in zip(arrays[1:], shifts)]


def exchange(array, axis):
    return lax.all_to_all(array, axis, 0, 0, tiled=True)


def on_device(hidden, queries, values, codes, exponents, base, momentum):
    x, c, z, y = (lax.axis_index(name) for name in ("x", "c", "zl", "y"))
    place = jnp.stack([c, z, y, x * NC + c]).astype(jnp.int32)

    delta, part = prep(codes[0], exponents[0], base)
    part_all = lax.all_gather(part, "y", axis=0, tiled=True)

    sent = exchange(delta, ("x", "c"))
    hidden_here = deal([hidden[0]], "zl")
    sent, hidden_here[1] = lax.optimization_barrier((sent, hidden_here[1]))
    eighth = jnp.sum(sent.astype(jnp.float32), axis=0).astype(jnp.bfloat16)
    pair = add(eighth, swap(eighth, "zh", [(0, 1), (2, 3)])).astype(jnp.bfloat16)
    swapped = swap(pair, "zh", [(1, 2), (3, 0)])
    both = deal([queries[0], values[0]], "zl")
    swapped, hidden_here[2], hidden_here[3], both[1] = lax.optimization_barrier(
        (swapped, hidden_here[2], hidden_here[3], both[1])
    )
    outer = outer_step(place, pair, swapped, base, momentum)

    same = exchange(outer, ("x", "y"))
    ordered, local = local_product(place, hidden_here, part_all)
    same, ordered, local, *both = lax.optimization_barrier((same, ordered, local, *both))
    other = lax.ppermute(same, "c", [(0, 1), (1, 0)])

    sums = project(place, ordered, local, same, other)
    sums, *both = lax.optimization_barrier((sums, *both))
    sums = exchange(sums, "zl")
    by_head = turn(list(regroup(place, both)), "y")
    blended = blend(place, delta, base, same, other)
    sums, blended, *by_head = lax.optimization_barrier((sums, blended, *by_head))
    keys = exchange(reduce_keys(sums), "y")
    mixed = exchange(attend(place, keys, by_head), ("zl", "y"))
    return blended[None], lay(mixed)[None]


def solution(mesh):
    split = Mesh(
        mesh.devices.reshape(NX, NZH, NC, NZL, NY),
        ("x", "zh", "c", "zl", "y"),
    )
    replica, fsdp = ("x", "zh", "c"), ("zl", "y")
    stacked = P(replica, fsdp, None)
    return jax.shard_map(
        on_device,
        mesh=split,
        in_specs=(stacked,) * 5 + (P(fsdp, None),) * 2,
        out_specs=(stacked, stacked),
        check_vma=False,
    )
```

```python
import math

import jax
import jax.numpy as jnp
from jax import lax
from jax.experimental import pallas as pl
from jax.experimental.pallas import tpu as pltpu
from jax.sharding import Mesh
from jax.sharding import PartitionSpec as P

D = 4608
HD = 128
QH = 16
KVH = 8
BLOCK = 128
KC = 1024
VMEM = pl.BlockSpec(memory_space=pltpu.VMEM)
SMEM = pl.BlockSpec(memory_space=pltpu.SMEM)
ANY = pl.BlockSpec(memory_space=pl.ANY)

momentum_rate = 0.9
outer_rate = 0.7
blend_share = 0.25
logit_cap = 50.0
query_scalar = 12.0

NX, NZH, NC, NZL, NY = 4, 4, 2, 4, 4


def params(mib=58):
    return pltpu.CompilerParams(vmem_limit_bytes=mib << 20)


def start_all(copies):
    for copy in copies:
        copy.start()
    return copies


def prep_kernel(codes_hbm, exps_ref, base_hbm, delta_ref, part_ref, codes, base, sems):
    half = codes.shape[0] // 2
    copies = []
    for i in range(2):
        rows = pl.ds(i * half, half)
        copies.append(pltpu.make_async_copy(codes_hbm.at[rows], codes.at[rows], sems.at[2 * i]))
        copies.append(pltpu.make_async_copy(base_hbm.at[rows], base.at[rows], sems.at[2 * i + 1]))
    start_all(copies)
    factor = jnp.exp2(exps_ref[...].astype(jnp.float32)).T
    for i in range(2):
        copies[2 * i].wait()
        copies[2 * i + 1].wait()
        rows = slice(i * half, (i + 1) * half)
        for j in range(KC // BLOCK):
            cols = slice(j * BLOCK, (j + 1) * BLOCK)
            delta = codes[rows, cols].astype(jnp.float32) * factor[rows, j : j + 1]
            delta_ref[j, rows] = delta.astype(jnp.bfloat16)
            part_ref[rows, cols] = (base[rows, cols].astype(jnp.float32) - delta).astype(
                jnp.bfloat16
            )


def prep(codes, exps, base):
    rows = codes.shape[0]
    return pl.pallas_call(
        prep_kernel,
        out_shape=(
            jax.ShapeDtypeStruct((KC // BLOCK, rows, BLOCK), jnp.bfloat16),
            jax.ShapeDtypeStruct((rows, KC), jnp.bfloat16),
        ),
        in_specs=[ANY, VMEM, ANY],
        out_specs=(VMEM, VMEM),
        scratch_shapes=[
            pltpu.VMEM((rows, KC), jnp.bfloat16),
            pltpu.VMEM((rows, KC), jnp.bfloat16),
            pltpu.SemaphoreType.DMA((4,)),
        ],
        compiler_params=params(),
        name="prep",
    )(codes, exps.T, base)


def step_kernel(place_ref, mine_ref, sent_ref, base_ref, momentum_ref, out_ref):
    mean = (mine_ref[...].astype(jnp.float32) + sent_ref[...].astype(jnp.float32)) * (
        1.0 / (NX * NZH * NC)
    )
    moment_new = momentum_rate * momentum_ref[...].astype(jnp.float32) + mean
    outer = base_ref[...].astype(jnp.float32) - outer_rate * (mean + momentum_rate * moment_new)
    outer = outer.astype(jnp.bfloat16)
    for i in range(out_ref.shape[0]):
        out_ref[i] = outer


def outer_step(place, mine, sent, base, momentum):
    rows = mine.shape[0]
    whole = pl.BlockSpec((rows, BLOCK), lambda i, p: (0, 0))
    block = pl.BlockSpec((rows, BLOCK), lambda i, p: (0, p[3]))
    return pl.pallas_call(
        step_kernel,
        out_shape=jax.ShapeDtypeStruct((NX * NY, rows, BLOCK), jnp.bfloat16),
        grid_spec=pltpu.PrefetchScalarGridSpec(
            num_scalar_prefetch=1,
            grid=(1,),
            in_specs=[whole, whole, block, block],
            out_specs=pl.BlockSpec((NX * NY, rows, BLOCK), lambda i, p: (0, 0, 0)),
        ),
        compiler_params=params(20),
        name="outer_step",
    )(place, mine, sent, base, momentum)


def local_kernel(place_ref, *refs):
    pieces, part_any, hidden_ref, out_ref, part, sems = refs[:4], *refs[4:]
    z = place_ref[1]
    copies = []
    for s in range(NZL):
        to = pl.ds(pl.multiple_of(lax.rem(z - s + NZL, NZL) * 128, 128), 128)
        copies.append(pltpu.make_async_copy(pieces[s], hidden_ref.at[to], sems.at[s]))
    step = part.shape[0] // NY
    for y in range(NY):
        rows = pl.ds(y * step, step)
        copies.append(pltpu.make_async_copy(part_any.at[rows], part.at[rows], sems.at[NZL + y]))
    for copy in start_all(copies):
        copy.wait()
    for n in range(NZL):
        cols = slice(n * 256, (n + 1) * 256)
        out_ref[n] = blend_share * jnp.dot(
            hidden_ref[...], part[:, cols], preferred_element_type=jnp.float32
        )


def local_product(place, hidden, part):
    depth = part.shape[0]
    return pl.pallas_call(
        local_kernel,
        out_shape=(
            jax.ShapeDtypeStruct((512, depth), jnp.bfloat16),
            jax.ShapeDtypeStruct((NZL, 512, 256), jnp.float32),
        ),
        in_specs=[SMEM] + [ANY] * 5,
        out_specs=(VMEM, VMEM),
        scratch_shapes=[
            pltpu.VMEM(part.shape, jnp.bfloat16),
            pltpu.SemaphoreType.DMA((2 * NZL,)),
        ],
        compiler_params=params(),
        name="local_product",
    )(place, *hidden, part)


def project_kernel(place_ref, hidden_any, local_any, same_any, other_any, out_ref, *refs):
    hidden, local, pieces, weight, sems, local_sems, hidden_sem = refs
    c = place_ref[0]
    hidden_copy = pltpu.make_async_copy(hidden_any, hidden, hidden_sem)
    copies = []
    for n in range(NZL):
        for near, source in enumerate((same_any, other_any)):
            copies.append(
                pltpu.make_async_copy(source.at[n], pieces.at[near, n], sems.at[near, n])
            )
        copies.append(pltpu.make_async_copy(local_any.at[n], local.at[n], local_sems.at[n]))
    start_all(copies[:2] + [hidden_copy] + copies[2:])
    for n in range(NZL):
        for near in range(NC):
            copies[3 * n + near].wait()
            at = pl.multiple_of(lax.rem(c + near, NC) * BLOCK, BLOCK)
            weight[n, :, pl.ds(at, BLOCK)] = pieces[near, n]
        if n == 0:
            hidden_copy.wait()
        outer = jnp.dot(hidden[...], weight[n], preferred_element_type=jnp.float32)
        copies[3 * n + 2].wait()
        out_ref[n] = (local[n] + (1.0 - blend_share) * outer).astype(jnp.bfloat16)


def project(place, hidden, local, same, other):
    depth = hidden.shape[1]
    blocks = (NZL, depth, BLOCK)
    return pl.pallas_call(
        project_kernel,
        out_shape=jax.ShapeDtypeStruct((NZL, 512, 2 * BLOCK), jnp.bfloat16),
        in_specs=[SMEM] + [ANY] * 4,
        out_specs=VMEM,
        scratch_shapes=[
            pltpu.VMEM(hidden.shape, jnp.bfloat16),
            pltpu.VMEM(local.shape, jnp.float32),
            pltpu.VMEM((NC,) + blocks, jnp.bfloat16),
            pltpu.VMEM((NZL, depth, 2 * BLOCK), jnp.bfloat16),
            pltpu.SemaphoreType.DMA((NC, NZL)),
            pltpu.SemaphoreType.DMA((NZL,)),
            pltpu.SemaphoreType.DMA,
        ],
        compiler_params=params(),
        name="project",
    )(place, hidden, local, same.reshape(blocks), other.reshape(blocks))


def reduce_kernel(sums_ref, out_ref):
    for head in range(2):
        cols = slice(head * HD, (head + 1) * HD)
        total = sums_ref[0, :, cols].astype(jnp.float32)
        for i in range(1, NZL):
            total += sums_ref[i, :, cols].astype(jnp.float32)
        keys = (total * (1.0 / math.sqrt(D))).astype(jnp.bfloat16)
        out_ref[2 * head] = keys
        out_ref[2 * head + 1] = keys


def reduce_keys(sums):
    return pl.pallas_call(
        reduce_kernel,
        out_shape=jax.ShapeDtypeStruct((NY, sums.shape[1], HD), jnp.bfloat16),
        in_specs=[VMEM],
        out_specs=VMEM,
        compiler_params=params(20),
        name="reduce_keys",
    )(sums)


def regroup_kernel(place_ref, *refs):
    pieces, outs, sems = refs[:4], refs[4:8], refs[8]
    z, y = place_ref[1], place_ref[2]
    copies = []
    for step in range(NY):
        to_y = lax.rem(y + step, NY)
        query_at = pl.multiple_of(to_y * HD, HD)
        value_at = pl.multiple_of(4 * HD + (to_y // 2) * HD, HD)
        for s in range(NZL):
            rows = pl.ds(pl.multiple_of(lax.rem(z - s + NZL, NZL) * 128, 128), 128)
            for i, at in enumerate((query_at, value_at)):
                copies.append(
                    pltpu.make_async_copy(
                        pieces[s].at[:, pl.ds(at, HD)],
                        outs[step].at[rows, pl.ds(i * HD, HD)],
                        sems.at[step, s, i],
                    )
                )
    for copy in start_all(copies):
        copy.wait()


def regroup(place, pieces):
    return pl.pallas_call(
        regroup_kernel,
        out_shape=[jax.ShapeDtypeStruct((512, 2 * HD), jnp.bfloat16)] * NY,
        in_specs=[SMEM] + [ANY] * 4,
        out_specs=[ANY] * NY,
        scratch_shapes=[pltpu.SemaphoreType.DMA((NY, NZL, 2))],
        compiler_params=params(20),
        name="regroup",
    )(place, *pieces)


def blend_kernel(place_ref, delta_ref, base_ref, same_ref, other_ref, out_ref):
    c = place_ref[0]
    for x in range(NX):
        for near, ref in enumerate((same_ref, other_ref)):
            j = x * NC + lax.rem(c + near, NC)
            cols = pl.ds(pl.multiple_of(j * BLOCK, BLOCK), BLOCK)
            mine = base_ref[:, cols].astype(jnp.float32) - delta_ref[j].astype(jnp.float32)
            outer = ref[x, 0].astype(jnp.float32)
            blend = blend_share * mine + (1.0 - blend_share) * outer
            out_ref[:, cols] = blend.astype(jnp.bfloat16)


def blend(place, delta, base, same, other):
    rows = base.shape[0]
    piece = pl.BlockSpec((NX, 1, rows, BLOCK), lambda i, p: (0, p[2], 0, 0))
    split = (NX, NY, rows, BLOCK)
    return pl.pallas_call(
        blend_kernel,
        out_shape=jax.ShapeDtypeStruct((rows, KC), jnp.bfloat16),
        grid_spec=pltpu.PrefetchScalarGridSpec(
            num_scalar_prefetch=1,
            grid=(1,),
            in_specs=[
                pl.BlockSpec(delta.shape, lambda i, p: (0, 0, 0)),
                pl.BlockSpec((rows, KC), lambda i, p: (0, 0)),
                piece,
                piece,
            ],
            out_specs=pl.BlockSpec((rows, KC), lambda i, p: (0, 0)),
        ),
        compiler_params=params(20),
        name="blend",
    )(place, delta, base, same.reshape(split), other.reshape(split))


def attend_kernel(place_ref, keys_any, *refs):
    pieces, (out_ref, queries, keys, values, sems) = refs[:4], refs[4:]
    y = place_ref[2]
    copies = [pltpu.make_async_copy(keys_any, keys, sems.at[0])]
    for i, target in enumerate((queries, values)):
        for s in range(NY):
            copies.append(
                pltpu.make_async_copy(
                    pieces[s].at[:, pl.ds(i * HD, HD)],
                    target.at[lax.rem(y - s + NY, NY)],
                    sems.at[1 + i * NY + s],
                )
            )
    start_all(copies)
    seen = lax.broadcasted_iota(jnp.int32, (256, 256), 1) <= lax.broadcasted_iota(
        jnp.int32, (256, 256), 0
    )
    for copy in copies:
        copy.wait()

    def pair(ref, z, at):
        return ref[2 * at : 2 * at + 2, z * 128 : (z + 1) * 128, :].reshape(256, HD)

    for at in range(2 * NZL):
        q = pair(queries, at // 2, at % 2)
        acc = jnp.zeros((256, HD), jnp.float32)
        total = jnp.zeros((256, 128), jnp.float32)
        for by in range(at + 1):
            scores = lax.dot_general(
                q,
                pair(keys, by // 2, by % 2),
                (((1,), (1,)), ((), ())),
                preferred_element_type=jnp.float32,
            )
            p = jnp.exp(logit_cap * jnp.tanh(scores * (1.0 / (query_scalar * logit_cap))))
            if by == at:
                p = jnp.where(seen, p, 0.0)
            total += p[:, :128] + p[:, 128:]
            acc += jnp.dot(
                p.astype(jnp.bfloat16),
                pair(values, by // 2, by % 2),
                preferred_element_type=jnp.float32,
            )
        out = (acc / jnp.sum(total, axis=1, keepdims=True)).astype(jnp.bfloat16)
        out_ref[2 * at] = out[:128]
        out_ref[2 * at + 1] = out[128:]


def attend(place, keys, pieces):
    whole = pltpu.VMEM((NY, 512, HD), jnp.bfloat16)
    return pl.pallas_call(
        attend_kernel,
        out_shape=jax.ShapeDtypeStruct((NZL * NY, 128, HD), jnp.bfloat16),
        in_specs=[SMEM] + [ANY] * 5,
        out_specs=VMEM,
        scratch_shapes=[whole, whole, whole, pltpu.SemaphoreType.DMA((1 + 2 * NY,))],
        compiler_params=params(20),
        name="attend",
    )(place, keys, *pieces)


def lay_kernel(mixed_any, out_any, sems):
    places, _, width = mixed_any.shape
    copies = []
    for i in range(places):
        cols = pl.ds(i * width, width)
        copies.append(pltpu.make_async_copy(mixed_any.at[i], out_any.at[:, cols], sems.at[i]))
    for copy in start_all(copies):
        copy.wait()


def lay(mixed):
    places, rows, width = mixed.shape
    return pl.pallas_call(
        lay_kernel,
        out_shape=jax.ShapeDtypeStruct((rows, places * width), jnp.bfloat16),
        in_specs=[ANY],
        out_specs=ANY,
        scratch_shapes=[pltpu.SemaphoreType.DMA((places,))],
        compiler_params=params(20),
        name="lay",
    )(mixed)


def swap(array, axis, pairs):
    return lax.ppermute(array, axis, pairs + [(b, a) for a, b in pairs])


def add(a, b):
    return a.astype(jnp.float32) + b.astype(jnp.float32)


def deal(arrays, axis):
    at = lax.axis_index(axis)
    pieces = []
    for step in range(4):
        to = lax.rem(at + step, 4)
        cut = []
        for array in arrays:
            width = array.shape[1] // 4
            cut.append(lax.dynamic_slice_in_dim(array, to * width, width, 1))
        piece = jnp.concatenate(cut, axis=1)
        if step:
            piece = lax.ppermute(piece, axis, [(i, (i + step) % 4) for i in range(4)])
        pieces.append(piece)
    return pieces


def turn(arrays, axis):
    shifts = [[(i, (i + step) % 4) for i in range(4)] for step in (1, 2, 3)]
    return arrays[:1] + [lax.ppermute(a, axis, shift) for a, shift in zip(arrays[1:], shifts)]


def exchange(array, axis):
    return lax.all_to_all(array, axis, 0, 0, tiled=True)


def on_device(hidden, queries, values, codes, exponents, base, momentum):
    x, c, z, y = (lax.axis_index(name) for name in ("x", "c", "zl", "y"))
    place = jnp.stack([c, z, y, x * NC + c]).astype(jnp.int32)

    delta, part = prep(codes[0], exponents[0], base)
    part_all = lax.all_gather(part, "y", axis=0, tiled=True)

    sent = exchange(delta, ("x", "c"))
    hidden_here = deal([hidden[0]], "zl")
    sent, hidden_here[1] = lax.optimization_barrier((sent, hidden_here[1]))
    eighth = jnp.sum(sent.astype(jnp.float32), axis=0).astype(jnp.bfloat16)
    pair = add(eighth, swap(eighth, "zh", [(0, 1), (2, 3)])).astype(jnp.bfloat16)
    pair, hidden_here[2] = lax.optimization_barrier((pair, hidden_here[2]))
    swapped = swap(pair, "zh", [(1, 2), (3, 0)])
    both = deal([queries[0], values[0]], "zl")
    swapped, hidden_here[3], both[1], both[3] = lax.optimization_barrier(
        (swapped, hidden_here[3], both[1], both[3])
    )
    outer = outer_step(place, pair, swapped, base, momentum)

    same = exchange(outer, ("x", "y"))
    ordered, local = local_product(place, hidden_here, part_all)
    same, ordered, local, *both = lax.optimization_barrier((same, ordered, local, *both))
    other = lax.ppermute(same, "c", [(0, 1), (1, 0)])

    sums = project(place, ordered, local, same, other)
    sums, *both = lax.optimization_barrier((sums, *both))
    sums = exchange(sums, "zl")
    by_head = turn(list(regroup(place, both)), "y")
    blended = blend(place, delta, base, same, other)
    sums, blended, *by_head = lax.optimization_barrier((sums, blended, *by_head))
    keys = exchange(reduce_keys(sums), "y")
    mixed = exchange(attend(place, keys, by_head), ("zl", "y"))
    return blended[None], lay(mixed)[None]


def solution(mesh):
    split = Mesh(
        mesh.devices.reshape(NX, NZH, NC, NZL, NY),
        ("x", "zh", "c", "zl", "y"),
    )
    replica, fsdp = ("x", "zh", "c"), ("zl", "y")
    stacked = P(replica, fsdp, None)
    return jax.shard_map(
        on_device,
        mesh=split,
        in_specs=(stacked,) * 5 + (P(fsdp, None),) * 2,
        out_specs=(stacked, stacked),
        check_vma=False,
    )
```
